32 devices in a mesh: row: 4 (over x, core), rhs: 8 (over z, y).
Axes of the slice: x: 2, y: 2, z: 4, core: 2. Of those that a mesh axis runs over, the one named last changes fastest.
Arguments:
- local_rhs: bfloat16 [168, 128, 1024], P('row', None, 'rhs'), may hold values from -6 to 6
- top_rhs: bfloat16 [4, 128, 1024], P('row', None, 'rhs'), may hold values from -6 to 6
- diag_inv: bfloat16 [168, 128, 128], P('row', 'rhs'), as said below
- top_inv: bfloat16 [4, 128, 128], P('row', 'rhs'), as said below
- off_blocks: bfloat16 [168, 4, 128, 128], P('row', None, 'rhs'), may hold values from -0.125 to 0.125
- top_factor: bfloat16 [4, 4, 128, 128], P('row', None, 'rhs'), may hold values from -0.25 to 0.25
- targets: int32 [168, 4], P('row'), may hold values from 24 to 45, as said below
Outputs:
- local_solution: bfloat16 [168, 128, 1024], P('row', None, 'rhs')
- top_solution: bfloat16 [4, 128, 1024], P('row', None, 'rhs')
The draws below stay inside these ranges and needn't reach their ends.
Inputs may be any that keep to these rules, and one draw needn't show every extreme that they name: `diag_inv`: each block is lower triangular. `top_inv`: each block is lower triangular. `targets`: row r * 42 + k holds 4 distinct codes; a code c < 42 names local supernode r * 42 + c, of a higher level than k; a code c >= 42 names top block c - 42.
All inputs are finite; a program needn't handle non-finite values.
Results may differ from the reference program's by a relative error of at most 0.023.
Values may be sent and summed in bfloat16 or wider, within the bound.
A program may use at most 64 MiB of HBM per device.

```python
import math
import jax
import jax.numpy as jnp
from jax import lax

B = 128
NB = 4
LEAF = 24
RHS_DEV = 128
SUB = 42
NLOC = 168
TOP = 4
NRHS = 1024
N_ROW = 4
N_RHS = 8


def lower_inverse(key, count):
    scales = jax.random.uniform(jax.random.fold_in(key, 11), (count, B), jnp.float32, 0.7, 1.3)
    noise = jax.random.normal(jax.random.fold_in(key, 12), (count, B, B), jnp.float32) * (0.6 / math.sqrt(B))
    lower = jnp.tril(noise, -1) + scales[:, :, None] * jnp.eye(B, dtype=jnp.float32)[None]
    return lower.astype(jnp.bfloat16)


def draw_diag_inv(key, part):
    return lower_inverse(key, SUB * N_ROW)


def draw_top_inv(key, part):
    return lower_inverse(key, N_ROW)


def draw_targets(key, part):
    cand_count = SUB + TOP
    local_index = jnp.arange(SUB, dtype=jnp.int32)
    next_level = jnp.where(local_index < LEAF, LEAF, jnp.where(local_index < LEAF + LEAF // 2, LEAF + LEAF // 2, SUB))
    candidate = jnp.arange(cand_count, dtype=jnp.int32)
    allowed = candidate[None, :] >= next_level[:, None]
    scores = jax.random.randint(jax.random.fold_in(key, 21), (N_ROW, SUB, cand_count), 0, 1 << 20, dtype=jnp.int32) * cand_count + candidate
    scores = jnp.where(allowed[None], scores, -1)
    chosen = lax.top_k(scores, NB)[1]
    return chosen.reshape(N_ROW * SUB, NB).astype(jnp.int32)


def level_of(key, shape, shards, least, high):
    factor_of, own = 1.0, jax.random.fold_in(key, 6)
    for dim, shards_of in shards:
        draws = jnp.exp(jax.random.uniform(jax.random.fold_in(own, dim), (shards_of,), jnp.float32, least / len(shards), high / len(shards)))
        factor_of = factor_of * jnp.repeat(draws, shape[dim] // shards_of).reshape([-1 if axis == dim else 1 for axis in range(len(shape))])
    return factor_of


def bell_draw(stream_key, extent, scale, bound, shards=(), kind=jnp.bfloat16):
    drawn = scale * jax.random.normal(stream_key, extent, jnp.float32)
    if shards:
        drawn = drawn * level_of(stream_key, extent, shards, -0.22, 0.18)
    return jnp.clip(drawn, -bound, bound).astype(kind)


def setup_inputs(seed: int = 0) -> dict:
    arg_keys = jax.random.split(jax.random.key(seed), 8)
    return {
        "local_rhs": bell_draw(arg_keys[0], (NLOC, B, NRHS), 1.0, 6.0, ((0, 4), (2, 8))),
        "top_rhs": bell_draw(arg_keys[1], (TOP, B, NRHS), 1.0, 6.0, ((0, 4), (2, 8))),
        "diag_inv": draw_diag_inv(jax.random.fold_in(arg_keys[7], 71), 0),
        "top_inv": draw_top_inv(jax.random.fold_in(arg_keys[7], 71), 0),
        "off_blocks": bell_draw(arg_keys[4], (NLOC, NB, B, B), (B * 16) ** -0.5, 0.125, ((0, 4), (2, 8))),
        "top_factor": bell_draw(arg_keys[5], (TOP, TOP, B, B), (B * TOP) ** -0.5, 0.25, ((0, 4), (2, 8))),
        "targets": draw_targets(jax.random.fold_in(arg_keys[7], 71), 0),
    }


def reference(local_rhs, top_rhs, diag_inv, top_inv, off_blocks, top_factor, targets):
    inverse = diag_inv.reshape(N_ROW, SUB, B, B).astype(jnp.float32)
    blocks = off_blocks.reshape(N_ROW, SUB, NB, B, B).astype(jnp.float32)
    codes = targets.reshape(N_ROW, SUB, NB).astype(jnp.int32)
    owner = jnp.broadcast_to(jnp.arange(N_ROW, dtype=jnp.int32)[:, None, None], codes.shape)
    level_ranges = ((0, LEAF), (LEAF, LEAF + LEAF // 2), (LEAF + LEAF // 2, SUB))

    def solve_panel(panel_args):
        local_panel, top_panel = panel_args
        rows_all = local_panel.reshape(N_ROW, SUB, B, RHS_DEV)
        acc_local = jnp.zeros((N_ROW, SUB, B, RHS_DEV), jnp.float32)
        acc_top = jnp.zeros((TOP, B, RHS_DEV), jnp.float32)
        solved = []
        for first_row, end_row in level_ranges:
            residual_rows = (rows_all[:, first_row:end_row].astype(jnp.float32) - acc_local[:, first_row:end_row]).astype(jnp.bfloat16)
            level_partial = jnp.einsum("rsab,rsbp->rsap", inverse[:, first_row:end_row], residual_rows.astype(jnp.float32)).astype(jnp.bfloat16)
            solved.append(level_partial)
            products = jnp.einsum("rsjab,rsbp->rsjap", blocks[:, first_row:end_row], level_partial.astype(jnp.float32))
            spread = jnp.zeros((N_ROW, SUB + TOP, B, RHS_DEV), jnp.float32)
            spread = spread.at[owner[:, first_row:end_row], codes[:, first_row:end_row]].add(products)
            acc_local = acc_local + spread[:, :SUB]
            acc_top = acc_top + jnp.sum(spread[:, SUB:], axis=0)
        top_values = []
        for step_index in range(TOP):
            carried = jnp.zeros((B, RHS_DEV), jnp.float32)
            for earlier in range(step_index):
                carried = carried + jnp.dot(top_factor[step_index, earlier], top_values[earlier], preferred_element_type=jnp.float32)
            residual_rows = ((top_panel[step_index].astype(jnp.float32) - acc_top[step_index]) - carried).astype(jnp.bfloat16)
            top_values.append(jnp.dot(top_inv[step_index], residual_rows, preferred_element_type=jnp.float32).astype(jnp.bfloat16))
        local_out = jnp.concatenate(solved, axis=1).reshape(NLOC, B, RHS_DEV)
        return local_out, jnp.stack(top_values)

    local_panels = local_rhs.reshape(NLOC, B, N_RHS, RHS_DEV).transpose(2, 0, 1, 3)
    top_panels = top_rhs.reshape(TOP, B, N_RHS, RHS_DEV).transpose(2, 0, 1, 3)
    local_out, top_out = lax.map(solve_panel, (local_panels, top_panels))
    local_solution = local_out.transpose(1, 2, 0, 3).reshape(NLOC, B, NRHS)
    top_solution = top_out.transpose(1, 2, 0, 3).reshape(TOP, B, NRHS)
    return local_solution, top_solution
```

```python
import functools
import jax
import jax.numpy as jnp
from jax import lax
from jax.experimental import pallas as pl
from jax.experimental.pallas import tpu as pltpu
from jax.sharding import PartitionSpec as P

LEAF = 24


def spread(shard, axis, root):
    mine = lax.axis_index(axis) == root
    return lax.psum(jnp.where(mine, shard, jnp.zeros_like(shard)), axis)


def local(local_rhs, top_rhs, diag_inv, top_inv, off_blocks, top_factor, targets):
    sub_count = local_rhs.shape[0]
    panel_width = local_rhs.shape[1]
    columns = local_rhs.shape[2]
    top_count = lax.axis_size("row")
    cand_count = sub_count + top_count
    acc_local = jnp.zeros((sub_count, panel_width, columns), jnp.float32)
    acc_top = jnp.zeros((top_count, panel_width, columns), jnp.float32)
    level_ranges = ((0, LEAF), (LEAF, LEAF + LEAF // 2), (LEAF + LEAF // 2, sub_count))
    solved = []
    for first_row, end_row in level_ranges:
        residual_rows = (
            local_rhs[first_row:end_row].astype(jnp.float32) - acc_local[first_row:end_row]
        ).astype(jnp.bfloat16)

        def apply_inverse(slice_part, offset, residual_rows=residual_rows):
            return jnp.einsum(
                "jxm,jme->jxe", slice_part, residual_rows, preferred_element_type=jnp.float32
            )

        level_partial = apply_inverse(
            lax.all_gather(diag_inv[first_row:end_row], "rhs", axis=1, tiled=True), jnp.int32(0)
        ).astype(jnp.bfloat16)
        solved.append(level_partial)
        target_codes = targets[first_row:end_row].reshape(-1)
        later_count = cand_count - end_row
        selector = (
            jnp.arange(later_count, dtype=jnp.int32)[:, None] == target_codes[None, :] - end_row
        ).astype(jnp.float32)

        def spread_updates(slice_part, offset, level_partial=level_partial, selector=selector):
            products = jnp.einsum(
                "yiko,yoq->yikq", slice_part, level_partial, preferred_element_type=jnp.float32
            )
            flattened = products.reshape(selector.shape[1], slice_part.shape[2], columns)
            return jnp.einsum("cn,nar->car", selector, flattened, precision=lax.Precision.HIGHEST)

        contrib = spread_updates(
            lax.all_gather(off_blocks[first_row:end_row], "rhs", axis=2, tiled=True), jnp.int32(0)
        )
        acc_local = acc_local.at[end_row:].add(contrib[: sub_count - end_row])
        acc_top = acc_top + contrib[sub_count - end_row :]
    inverse_rows = top_inv.reshape(1, 1, top_inv.shape[1], panel_width)
    top_full, inv_full = (
        lax.all_gather(top_factor, "rhs", axis=2, tiled=True),
        lax.all_gather(inverse_rows, "rhs", axis=2, tiled=True),
    )
    position = lax.axis_index("row")
    own_sum = lax.psum_scatter(
        acc_top.astype(jnp.bfloat16), "row", scatter_dimension=0, tiled=True
    ).astype(jnp.float32)
    base_value = top_rhs[0].astype(jnp.float32) - own_sum[0]

    def top_step(step_index, carry):
        carried, own_solution = carry
        residual_rows = (base_value - carried).astype(jnp.bfloat16)
        candidate = jnp.dot(
            inv_full[0, 0], residual_rows, preferred_element_type=jnp.float32
        ).astype(jnp.bfloat16)
        solution = spread(candidate, "row", step_index)
        own_solution = jnp.where(position == step_index, solution, own_solution)
        coupling_matrix = lax.dynamic_index_in_dim(top_full[0], step_index, 0, keepdims=False)
        update = jnp.dot(coupling_matrix, solution, preferred_element_type=jnp.float32)
        carried = carried + jnp.where(step_index < position, update, 0.0)
        return (carried, own_solution)

    initial_state = (
        jnp.zeros((panel_width, columns), jnp.float32),
        jnp.zeros((panel_width, columns), jnp.bfloat16),
    )
    own_separator = lax.fori_loop(0, top_count, top_step, initial_state)[1][None]
    return (jnp.concatenate(solved, axis=0), own_separator)


CHUNK = 3
LINE = 4
LEFT, RIGHT, ACROSS = 0, 1, 2
MESH = pl.DeviceIdType.MESH


def detour(k):
    return lax.rem(k, 6) == 3


def relay_kernel(
    rows, rhs_hbm, top_rhs_hbm, diag_hbm, top_inv_hbm, off_hbm, top_factor_hbm, targets,
    out_hbm, top_out_hbm,
    held, held_top, rhs, top_rhs, sol, acc, prod, part, parts, top_sol,
    load_sem, out_sem, send_sem, recv_sem, row_send, row_recv,
):
    sub, width, columns = rhs.shape
    chunks = 1 + sub // CHUNK
    cand = sub + rows
    row, me = lax.axis_index("row"), lax.axis_index("rhs")
    z, y = me // 2, lax.rem(me, 2)
    targets_of = {LEFT: me - 2, RIGHT: me + 2, ACROSS: z * 2 + 1 - y}
    peers = [lax.rem(row + p, rows) for p in range(1, rows)]

    loads = [
        pltpu.make_async_copy(top_inv_hbm.at[0], held_top.at[row, me, 0], load_sem.at[0]),
        pltpu.make_async_copy(top_factor_hbm.at[0], held_top.at[row, me, pl.ds(1, 4)], load_sem.at[1]),
        pltpu.make_async_copy(diag_hbm, held.at[me, :, 0], load_sem.at[2]),
        pltpu.make_async_copy(off_hbm, held.at[me, :, pl.ds(1, 4)], load_sem.at[3]),
        pltpu.make_async_copy(top_rhs_hbm.at[0], top_rhs.at[row], load_sem.at[4]),
        pltpu.make_async_copy(rhs_hbm, rhs, load_sem.at[5]),
    ]
    for load in loads:
        load.start()

    barrier = pltpu.get_barrier_semaphore()
    for peer in peers:
        pl.semaphore_signal(barrier, inc=1, device_id=(peer, me), device_id_type=MESH)
    pl.semaphore_signal(barrier, inc=1, device_id=(row, targets_of[ACROSS]), device_id_type=MESH)

    @pl.when(z > 0)
    def _():
        pl.semaphore_signal(barrier, inc=1, device_id=(row, targets_of[LEFT]), device_id_type=MESH)

    @pl.when(z < LINE - 1)
    def _():
        pl.semaphore_signal(barrier, inc=1, device_id=(row, targets_of[RIGHT]), device_id_type=MESH)

    def clear(c, carry):
        acc[c] = jnp.zeros((width, columns), jnp.float32)
        return carry

    lax.fori_loop(0, cand, clear, 0)
    for u in range(CHUNK):
        prod[u * 5 + 4] = jnp.zeros((width, columns), jnp.float32)

    ends = jnp.where(z == 0, 1, 0) + jnp.where(z == LINE - 1, 1, 0)
    pl.semaphore_wait(barrier, rows + 2 - ends)
    for load in loads:
        load.wait()

    def row_copy(kind, p, src, dst):
        return pltpu.make_async_remote_copy(
            src_ref=src, dst_ref=dst, send_sem=row_send.at[kind, p], recv_sem=row_recv.at[kind, row],
            device_id=(peers[p], me), device_id_type=MESH,
        )

    def row_arrival(kind, p, dst):
        return pltpu.make_async_remote_copy(
            src_ref=dst, dst_ref=dst, send_sem=row_send.at[kind, p], recv_sem=row_recv.at[kind, peers[p]],
            device_id=(peers[p], me), device_id_type=MESH,
        )

    for p in range(rows - 1):
        row_copy(0, p, top_rhs.at[row], top_rhs.at[row]).start()

    def either(k, src, count, act):
        @pl.when(k == 0)
        def _():
            act(held_top.at[row, pl.ds(src, count)])

        @pl.when(k > 0)
        def _():
            act(held.at[pl.ds(src, count), pl.ds((k - 1) * CHUNK, CHUNK)])

    def describe(ref, k, src, way):
        return pltpu.make_async_remote_copy(
            src_ref=ref, dst_ref=ref, send_sem=send_sem.at[way, k], recv_sem=recv_sem.at[k, src],
            device_id=(row, targets_of[way]), device_id_type=MESH,
        )

    def relay(k, src, wait, ways):
        def act(ref):
            if wait:
                describe(ref, k, src, ACROSS).wait_recv()
            for way, wanted in ways:
                @pl.when(wanted)
                def _(way=way):
                    describe(ref, k, src, way).start()

        either(k, src, 1, act)

    def drain(k):
        around = detour(k)
        sends = {
            LEFT: jnp.where(z > 0, (LINE - z) * jnp.where(around, 2, 1), 0),
            RIGHT: jnp.where(z < LINE - 1, (z + 1) * jnp.where(around, 2, 1), 0),
            ACROSS: jnp.where(around, 1, LINE),
        }
        for way, sizes in ((LEFT, (1, 2, 3, 4, 6)), (RIGHT, (1, 2, 3, 4, 6)), (ACROSS, (1, LINE))):
            for size in sizes:
                @pl.when(sends[way] == size)
                def _(way=way, size=size):
                    either(k, 0, size, lambda ref: describe(ref, k, 0, way).wait_send())

    def solve(k):
        first = (k - 1) * CHUNK
        half = LEAF + LEAF // 2
        codes = [[targets[first + u, j] for j in range(4)] for u in range(CHUNK)]
        for u in range(CHUNK):
            s = first + u
            residual = (rhs[s].astype(jnp.float32) - acc[s]).astype(jnp.bfloat16)
            inverse = held[:, s, 0].reshape(width, width)
            x = jnp.dot(inverse, residual, preferred_element_type=jnp.float32).astype(jnp.bfloat16)
            sol[s] = x
            blocks = jnp.concatenate([held[:, s, 1 + j].reshape(width, width) for j in range(4)], axis=0)
            prod[pl.ds(u * 5, 4)] = jnp.dot(blocks, x, preferred_element_type=jnp.float32).reshape(4, width, columns)
        pltpu.make_async_copy(sol.at[pl.ds(first, CHUNK)], out_hbm.at[pl.ds(first, CHUNK)], out_sem.at[0]).start()

        def add(c, carry):
            total = acc[c]
            for u in range(CHUNK):
                slot = jnp.int32(u * 5 + 4)
                for j in range(4):
                    slot = jnp.where(codes[u][j] == c, u * 5 + j, slot)
                total = total + prod[slot]
            acc[c] = total
            return carry

        lax.fori_loop(jnp.where(first < LEAF, LEAF, jnp.where(first < half, half, sub)), cand, add, 0)

    def step(i, carry):
        for lag in range(LINE + 1):
            k = i - lag

            @pl.when((k >= 0) & (k < chunks))
            def _(k=k, lag=lag):
                around = detour(k)
                if lag == 0:
                    relay(k, me, False, ((LEFT, z > 0), (RIGHT, z < LINE - 1), (ACROSS, z >= 0)))
                elif lag < LINE:
                    @pl.when(z >= lag)
                    def _():
                        relay(k, me - 2 * lag, True, ((RIGHT, z < LINE - 1), (ACROSS, jnp.logical_not(around))))

                    @pl.when(z + lag < LINE)
                    def _():
                        relay(k, me + 2 * lag, True, ((LEFT, z > 0), (ACROSS, jnp.logical_not(around))))

                @pl.when(around)
                def _():
                    far, d = targets_of[ACROSS], lag - 1
                    if d == 0:
                        relay(k, far, True, ((LEFT, z > 0), (RIGHT, z < LINE - 1)))
                    elif d > 0:
                        @pl.when(z >= d)
                        def _():
                            relay(k, far - 2 * d, True, ((RIGHT, z < LINE - 1),))

                        @pl.when(z + d < LINE)
                        def _():
                            relay(k, far + 2 * d, True, ((LEFT, z > 0),))

        k = i - LINE - 1

        @pl.when(k >= 0)
        def _():
            @pl.when(jnp.logical_not(detour(k)))
            def _():
                for other in range(LINE):
                    relay(k, other * 2 + 1 - y, True, ())

            @pl.when(k == 0)
            def _():
                for p in range(rows - 1):
                    row_copy(1, p, held_top.at[row], held_top.at[row]).start()

            @pl.when(k > 0)
            def _():
                solve(k)

        @pl.when(i >= 2 * LINE)
        def _():
            drain(i - 2 * LINE)

        return carry

    steps = chunks + LINE + 1
    lax.fori_loop(0, steps, step, 0)

    part[...] = acc[pl.ds(sub, rows)].astype(jnp.bfloat16)
    for p in range(rows - 1):
        row_copy(2, p, part, parts.at[row]).start()

    def drain_rest(k, carry):
        drain(k)
        return carry

    lax.fori_loop(steps - 2 * LINE, chunks, drain_rest, 0)
    for p in range(rows - 1):
        row_copy(0, p, top_rhs.at[row], top_rhs.at[row]).wait_send()
        row_copy(1, p, held_top.at[row], held_top.at[row]).wait_send()
        row_arrival(0, p, top_rhs.at[peers[p]]).wait_recv()
        row_arrival(1, p, held_top.at[peers[p]]).wait_recv()
    pltpu.make_async_copy(sol, out_hbm, out_sem.at[0]).wait()
    for p in range(rows - 1):
        row_arrival(2, p, parts.at[peers[p]]).wait_recv()

    for t in range(rows):
        base = acc[sub + t]
        for p in range(rows - 1):
            base = base + parts[peers[p], t].astype(jnp.float32)
        base = top_rhs[t].astype(jnp.float32) - base
        for earlier in range(t):
            factor = held_top[t, :, 1 + earlier].reshape(width, width)
            base = base - jnp.dot(factor, top_sol[earlier], preferred_element_type=jnp.float32)
        inverse = held_top[t, :, 0].reshape(width, width)
        top_sol[t] = jnp.dot(inverse, base.astype(jnp.bfloat16), preferred_element_type=jnp.float32).astype(jnp.bfloat16)
    last = pltpu.make_async_copy(top_sol.at[row], top_out_hbm.at[0], out_sem.at[1])
    last.start()
    for p in range(rows - 1):
        row_copy(2, p, part, parts.at[row]).wait_send()
    last.wait()


def relayed(local_rhs, top_rhs, diag_inv, top_inv, off_blocks, top_factor, targets):
    rows, ranks = lax.axis_size("row"), lax.axis_size("rhs")
    sub, width, columns = local_rhs.shape
    share = diag_inv.shape[1]
    chunks = 1 + sub // CHUNK
    bf16, f32 = jnp.bfloat16, jnp.float32
    return pl.pallas_call(
        functools.partial(relay_kernel, rows),
        out_shape=(
            jax.ShapeDtypeStruct(local_rhs.shape, bf16),
            jax.ShapeDtypeStruct(top_rhs.shape, bf16),
        ),
        in_specs=[pl.BlockSpec(memory_space=pl.ANY)] * 6 + [pl.BlockSpec(memory_space=pltpu.SMEM)],
        out_specs=(pl.BlockSpec(memory_space=pl.ANY),) * 2,
        scratch_shapes=[
            pltpu.VMEM((ranks, sub, 5, share, width), bf16),
            pltpu.VMEM((rows, ranks, 5, share, width), bf16),
            pltpu.VMEM((sub, width, columns), bf16),
            pltpu.VMEM((rows, width, columns), bf16),
            pltpu.VMEM((sub, width, columns), bf16),
            pltpu.VMEM((sub + rows, width, columns), f32),
            pltpu.VMEM((5 * CHUNK, width, columns), f32),
            pltpu.VMEM((rows, width, columns), bf16),
            pltpu.VMEM((rows, rows, width, columns), bf16),
            pltpu.VMEM((rows, width, columns), bf16),
            pltpu.SemaphoreType.DMA((6,)),
            pltpu.SemaphoreType.DMA((2,)),
            pltpu.SemaphoreType.DMA((3, chunks)),
            pltpu.SemaphoreType.DMA((chunks, ranks)),
            pltpu.SemaphoreType.DMA((3, rows - 1)),
            pltpu.SemaphoreType.DMA((3, rows)),
        ],
        compiler_params=pltpu.CompilerParams(
            collective_id=0, has_side_effects=True, vmem_limit_bytes=40 * 1024 * 1024
        ),
        cost_estimate=pl.CostEstimate(
            flops=10 * sub * width * width * columns, bytes_accessed=4 * local_rhs.size + 2 * off_blocks.size, transcendentals=0
        ),
    )(local_rhs, top_rhs, diag_inv, top_inv, off_blocks, top_factor, targets)


def solution(mesh):
    in_specs = (
        P("row", None, "rhs"),
        P("row", None, "rhs"),
        P("row", "rhs", None),
        P("row", "rhs", None),
        P("row", None, "rhs", None),
        P("row", None, "rhs", None),
        P("row", None),
    )
    out_specs = (P("row", None, "rhs"), P("row", None, "rhs"))
    body = relayed if mesh.shape["rhs"] == 2 * LINE else local
    return jax.shard_map(body, mesh=mesh, in_specs=in_specs, out_specs=out_specs, check_vma=False)
```

```python
import functools
import jax
import jax.numpy as jnp
from jax import lax
from jax.experimental import pallas as pl
from jax.experimental.pallas import tpu as pltpu
from jax.sharding import PartitionSpec as P

LEAF = 24


def spread(shard, axis, root):
    mine = lax.axis_index(axis) == root
    return lax.psum(jnp.where(mine, shard, jnp.zeros_like(shard)), axis)


def local(local_rhs, top_rhs, diag_inv, top_inv, off_blocks, top_factor, targets):
    sub_count = local_rhs.shape[0]
    panel_width = local_rhs.shape[1]
    columns = local_rhs.shape[2]
    top_count = lax.axis_size("row")
    cand_count = sub_count + top_count
    acc_local = jnp.zeros((sub_count, panel_width, columns), jnp.float32)
    acc_top = jnp.zeros((top_count, panel_width, columns), jnp.float32)
    level_ranges = ((0, LEAF), (LEAF, LEAF + LEAF // 2), (LEAF + LEAF // 2, sub_count))
    solved = []
    for first_row, end_row in level_ranges:
        residual_rows = (
            local_rhs[first_row:end_row].astype(jnp.float32) - acc_local[first_row:end_row]
        ).astype(jnp.bfloat16)

        def apply_inverse(slice_part, offset, residual_rows=residual_rows):
            return jnp.einsum(
                "jxm,jme->jxe", slice_part, residual_rows, preferred_element_type=jnp.float32
            )

        level_partial = apply_inverse(
            lax.all_gather(diag_inv[first_row:end_row], "rhs", axis=1, tiled=True), jnp.int32(0)
        ).astype(jnp.bfloat16)
        solved.append(level_partial)
        target_codes = targets[first_row:end_row].reshape(-1)
        later_count = cand_count - end_row
        selector = (
            jnp.arange(later_count, dtype=jnp.int32)[:, None] == target_codes[None, :] - end_row
        ).astype(jnp.float32)

        def spread_updates(slice_part, offset, level_partial=level_partial, selector=selector):
            products = jnp.einsum(
                "yiko,yoq->yikq", slice_part, level_partial, preferred_element_type=jnp.float32
            )
            flattened = products.reshape(selector.shape[1], slice_part.shape[2], columns)
            return jnp.einsum("cn,nar->car", selector, flattened, precision=lax.Precision.HIGHEST)

        contrib = spread_updates(
            lax.all_gather(off_blocks[first_row:end_row], "rhs", axis=2, tiled=True), jnp.int32(0)
        )
        acc_local = acc_local.at[end_row:].add(contrib[: sub_count - end_row])
        acc_top = acc_top + contrib[sub_count - end_row :]
    inverse_rows = top_inv.reshape(1, 1, top_inv.shape[1], panel_width)
    top_full, inv_full = (
        lax.all_gather(top_factor, "rhs", axis=2, tiled=True),
        lax.all_gather(inverse_rows, "rhs", axis=2, tiled=True),
    )
    position = lax.axis_index("row")
    own_sum = lax.psum_scatter(
        acc_top.astype(jnp.bfloat16), "row", scatter_dimension=0, tiled=True
    ).astype(jnp.float32)
    base_value = top_rhs[0].astype(jnp.float32) - own_sum[0]

    def top_step(step_index, carry):
        carried, own_solution = carry
        residual_rows = (base_value - carried).astype(jnp.bfloat16)
        candidate = jnp.dot(
            inv_full[0, 0], residual_rows, preferred_element_type=jnp.float32
        ).astype(jnp.bfloat16)
        solution = spread(candidate, "row", step_index)
        own_solution = jnp.where(position == step_index, solution, own_solution)
        coupling_matrix = lax.dynamic_index_in_dim(top_full[0], step_index, 0, keepdims=False)
        update = jnp.dot(coupling_matrix, solution, preferred_element_type=jnp.float32)
        carried = carried + jnp.where(step_index < position, update, 0.0)
        return (carried, own_solution)

    initial_state = (
        jnp.zeros((panel_width, columns), jnp.float32),
        jnp.zeros((panel_width, columns), jnp.bfloat16),
    )
    own_separator = lax.fori_loop(0, top_count, top_step, initial_state)[1][None]
    return (jnp.concatenate(solved, axis=0), own_separator)


CHUNK = 3
LINE = 4
LEFT, RIGHT, ACROSS = 0, 1, 2
MESH = pl.DeviceIdType.MESH


def detour(k):
    return lax.rem(k, 6) == 3


def relay_kernel(
    rows, rhs_hbm, top_rhs_hbm, diag_hbm, top_inv_hbm, off_hbm, top_factor_hbm, targets,
    out_hbm, top_out_hbm,
    held, held_top, rhs, top_rhs, sol, acc, prod, part, parts, top_sol,
    load_sem, out_sem, send_sem, recv_sem, row_send, row_recv,
):
    sub, width, columns = rhs.shape
    chunks = 1 + sub // CHUNK
    cand = sub + rows
    row, me = lax.axis_index("row"), lax.axis_index("rhs")
    z, y = me // 2, lax.rem(me, 2)
    targets_of = {LEFT: me - 2, RIGHT: me + 2, ACROSS: z * 2 + 1 - y}
    peers = [lax.rem(row + p, rows) for p in range(1, rows)]

    def load(index, src, dst):
        return pltpu.make_async_copy(src, dst, load_sem.at[index])

    early, late = pl.ds(0, CHUNK), pl.ds(CHUNK, sub - CHUNK)
    first_loads = [
        load(0, top_inv_hbm.at[0], held_top.at[row, me, 0]),
        load(1, top_factor_hbm.at[0], held_top.at[row, me, pl.ds(1, 4)]),
        load(2, diag_hbm.at[early], held.at[me, early, 0]),
        load(3, off_hbm.at[early], held.at[me, early, pl.ds(1, 4)]),
        load(4, top_rhs_hbm.at[0], top_rhs.at[row]),
    ]
    next_loads = [
        load(5, diag_hbm.at[late], held.at[me, late, 0]),
        load(6, off_hbm.at[late], held.at[me, late, pl.ds(1, 4)]),
    ]
    rhs_load = load(7, rhs_hbm, rhs)

    barrier = pltpu.get_barrier_semaphore()
    for peer in peers:
        pl.semaphore_signal(barrier, inc=1, device_id=(peer, me), device_id_type=MESH)
    pl.semaphore_signal(barrier, inc=1, device_id=(row, targets_of[ACROSS]), device_id_type=MESH)

    @pl.when(z > 0)
    def _():
        pl.semaphore_signal(barrier, inc=1, device_id=(row, targets_of[LEFT]), device_id_type=MESH)

    @pl.when(z < LINE - 1)
    def _():
        pl.semaphore_signal(barrier, inc=1, device_id=(row, targets_of[RIGHT]), device_id_type=MESH)

    for copy in first_loads + next_loads + [rhs_load]:
        copy.start()

    def clear(c, carry):
        acc[c] = jnp.zeros((width, columns), jnp.float32)
        return carry

    lax.fori_loop(0, cand, clear, 0)
    for u in range(CHUNK):
        prod[u * 5 + 4] = jnp.zeros((width, columns), jnp.float32)

    ends = jnp.where(z == 0, 1, 0) + jnp.where(z == LINE - 1, 1, 0)
    pl.semaphore_wait(barrier, rows + 2 - ends)
    for copy in first_loads:
        copy.wait()

    def row_copy(kind, p, src, dst):
        return pltpu.make_async_remote_copy(
            src_ref=src, dst_ref=dst, send_sem=row_send.at[kind, p], recv_sem=row_recv.at[kind, row],
            device_id=(peers[p], me), device_id_type=MESH,
        )

    def row_arrival(kind, p, dst):
        return pltpu.make_async_remote_copy(
            src_ref=dst, dst_ref=dst, send_sem=row_send.at[kind, p], recv_sem=row_recv.at[kind, peers[p]],
            device_id=(peers[p], me), device_id_type=MESH,
        )

    for p in range(rows - 1):
        row_copy(0, p, top_rhs.at[row], top_rhs.at[row]).start()

    def either(k, src, count, act):
        @pl.when(k == 0)
        def _():
            act(held_top.at[row, pl.ds(src, count)])

        @pl.when(k > 0)
        def _():
            act(held.at[pl.ds(src, count), pl.ds((k - 1) * CHUNK, CHUNK)])

    def describe(ref, k, src, way):
        return pltpu.make_async_remote_copy(
            src_ref=ref, dst_ref=ref, send_sem=send_sem.at[way, k], recv_sem=recv_sem.at[k, src],
            device_id=(row, targets_of[way]), device_id_type=MESH,
        )

    def relay(k, src, wait, ways):
        def act(ref):
            if wait:
                describe(ref, k, src, ACROSS).wait_recv()
            for way, wanted in ways:
                @pl.when(wanted)
                def _(way=way):
                    describe(ref, k, src, way).start()

        either(k, src, 1, act)

    def drain(k):
        around = detour(k)
        sends = {
            LEFT: jnp.where(z > 0, (LINE - z) * jnp.where(around, 2, 1), 0),
            RIGHT: jnp.where(z < LINE - 1, (z + 1) * jnp.where(around, 2, 1), 0),
            ACROSS: jnp.where(around, 1, LINE),
        }
        for way, sizes in ((LEFT, (1, 2, 3, 4, 6)), (RIGHT, (1, 2, 3, 4, 6)), (ACROSS, (1, LINE))):
            for size in sizes:
                @pl.when(sends[way] == size)
                def _(way=way, size=size):
                    either(k, 0, size, lambda ref: describe(ref, k, 0, way).wait_send())

    def solve(k):
        first = (k - 1) * CHUNK
        half = LEAF + LEAF // 2
        codes = [[targets[first + u, j] for j in range(4)] for u in range(CHUNK)]
        for u in range(CHUNK):
            s = first + u
            residual = (rhs[s].astype(jnp.float32) - acc[s]).astype(jnp.bfloat16)
            inverse = held[:, s, 0].reshape(width, width)
            x = jnp.dot(inverse, residual, preferred_element_type=jnp.float32).astype(jnp.bfloat16)
            sol[s] = x
            blocks = jnp.concatenate([held[:, s, 1 + j].reshape(width, width) for j in range(4)], axis=0)
            prod[pl.ds(u * 5, 4)] = jnp.dot(blocks, x, preferred_element_type=jnp.float32).reshape(4, width, columns)
        pltpu.make_async_copy(sol.at[pl.ds(first, CHUNK)], out_hbm.at[pl.ds(first, CHUNK)], out_sem.at[0]).start()

        def add(c, carry):
            total = acc[c]
            for u in range(CHUNK):
                slot = jnp.int32(u * 5 + 4)
                for j in range(4):
                    slot = jnp.where(codes[u][j] == c, u * 5 + j, slot)
                total = total + prod[slot]
            acc[c] = total
            return carry

        lax.fori_loop(jnp.where(first < LEAF, LEAF, jnp.where(first < half, half, sub)), cand, add, 0)

    def step(i, carry):
        for lag in range(LINE + 1):
            k = i - lag

            @pl.when((k >= 0) & (k < chunks))
            def _(k=k, lag=lag):
                around = detour(k)
                if lag == 0:
                    @pl.when(k == 2)
                    def _():
                        for copy in next_loads:
                            copy.wait()

                    relay(k, me, False, ((LEFT, z > 0), (RIGHT, z < LINE - 1), (ACROSS, z >= 0)))
                elif lag < LINE:
                    @pl.when(z >= lag)
                    def _():
                        relay(k, me - 2 * lag, True, ((RIGHT, z < LINE - 1), (ACROSS, jnp.logical_not(around))))

                    @pl.when(z + lag < LINE)
                    def _():
                        relay(k, me + 2 * lag, True, ((LEFT, z > 0), (ACROSS, jnp.logical_not(around))))

                @pl.when(around)
                def _():
                    far, d = targets_of[ACROSS], lag - 1
                    if d == 0:
                        relay(k, far, True, ((LEFT, z > 0), (RIGHT, z < LINE - 1)))
                    elif d > 0:
                        @pl.when(z >= d)
                        def _():
                            relay(k, far - 2 * d, True, ((RIGHT, z < LINE - 1),))

                        @pl.when(z + d < LINE)
                        def _():
                            relay(k, far + 2 * d, True, ((LEFT, z > 0),))

        k = i - LINE - 1

        @pl.when(k >= 0)
        def _():
            @pl.when(jnp.logical_not(detour(k)))
            def _():
                for other in range(LINE):
                    relay(k, other * 2 + 1 - y, True, ())

            @pl.when(k == 0)
            def _():
                rhs_load.wait()
                for p in range(rows - 1):
                    row_copy(1, p, held_top.at[row], held_top.at[row]).start()

            @pl.when(k > 0)
            def _():
                solve(k)

        @pl.when(i >= 2 * LINE)
        def _():
            drain(i - 2 * LINE)

        return carry

    steps = chunks + LINE + 1
    lax.fori_loop(0, steps, step, 0)

    part[...] = acc[pl.ds(sub, rows)].astype(jnp.bfloat16)
    for p in range(rows - 1):
        row_copy(2, p, part, parts.at[row]).start()

    def drain_rest(k, carry):
        drain(k)
        return carry

    lax.fori_loop(steps - 2 * LINE, chunks, drain_rest, 0)
    for p in range(rows - 1):
        row_copy(0, p, top_rhs.at[row], top_rhs.at[row]).wait_send()
        row_copy(1, p, held_top.at[row], held_top.at[row]).wait_send()
        row_arrival(0, p, top_rhs.at[peers[p]]).wait_recv()
        row_arrival(1, p, held_top.at[peers[p]]).wait_recv()
    pltpu.make_async_copy(sol, out_hbm, out_sem.at[0]).wait()
    for p in range(rows - 1):
        row_arrival(2, p, parts.at[peers[p]]).wait_recv()

    for t in range(rows):
        base = acc[sub + t]
        for p in range(rows - 1):
            base = base + parts[peers[p], t].astype(jnp.float32)
        base = top_rhs[t].astype(jnp.float32) - base
        for earlier in range(t):
            factor = held_top[t, :, 1 + earlier].reshape(width, width)
            base = base - jnp.dot(factor, top_sol[earlier], preferred_element_type=jnp.float32)
        inverse = held_top[t, :, 0].reshape(width, width)
        top_sol[t] = jnp.dot(inverse, base.astype(jnp.bfloat16), preferred_element_type=jnp.float32).astype(jnp.bfloat16)
    last = pltpu.make_async_copy(top_sol.at[row], top_out_hbm.at[0], out_sem.at[1])
    last.start()
    for p in range(rows - 1):
        row_copy(2, p, part, parts.at[row]).wait_send()
    last.wait()


def relayed(local_rhs, top_rhs, diag_inv, top_inv, off_blocks, top_factor, targets):
    rows, ranks = lax.axis_size("row"), lax.axis_size("rhs")
    sub, width, columns = local_rhs.shape
    share = diag_inv.shape[1]
    chunks = 1 + sub // CHUNK
    bf16, f32 = jnp.bfloat16, jnp.float32
    return pl.pallas_call(
        functools.partial(relay_kernel, rows),
        out_shape=(
            jax.ShapeDtypeStruct(local_rhs.shape, bf16),
            jax.ShapeDtypeStruct(top_rhs.shape, bf16),
        ),
        in_specs=[pl.BlockSpec(memory_space=pl.ANY)] * 6 + [pl.BlockSpec(memory_space=pltpu.SMEM)],
        out_specs=(pl.BlockSpec(memory_space=pl.ANY),) * 2,
        scratch_shapes=[
            pltpu.VMEM((ranks, sub, 5, share, width), bf16),
            pltpu.VMEM((rows, ranks, 5, share, width), bf16),
            pltpu.VMEM((sub, width, columns), bf16),
            pltpu.VMEM((rows, width, columns), bf16),
            pltpu.VMEM((sub, width, columns), bf16),
            pltpu.VMEM((sub + rows, width, columns), f32),
            pltpu.VMEM((5 * CHUNK, width, columns), f32),
            pltpu.VMEM((rows, width, columns), bf16),
            pltpu.VMEM((rows, rows, width, columns), bf16),
            pltpu.VMEM((rows, width, columns), bf16),
            pltpu.SemaphoreType.DMA((8,)),
            pltpu.SemaphoreType.DMA((2,)),
            pltpu.SemaphoreType.DMA((3, chunks)),
            pltpu.SemaphoreType.DMA((chunks, ranks)),
            pltpu.SemaphoreType.DMA((3, rows - 1)),
            pltpu.SemaphoreType.DMA((3, rows)),
        ],
        compiler_params=pltpu.CompilerParams(
            collective_id=0, has_side_effects=True, vmem_limit_bytes=60 * 1024 * 1024
        ),
        cost_estimate=pl.CostEstimate(
            flops=10 * sub * width * width * columns, bytes_accessed=4 * local_rhs.size + 2 * off_blocks.size, transcendentals=0
        ),
    )(local_rhs, top_rhs, diag_inv, top_inv, off_blocks, top_factor, targets)


def solution(mesh):
    in_specs = (
        P("row", None, "rhs"),
        P("row", None, "rhs"),
        P("row", "rhs", None),
        P("row", "rhs", None),
        P("row", None, "rhs", None),
        P("row", None, "rhs", None),
        P("row", None),
    )
    out_specs = (P("row", None, "rhs"), P("row", None, "rhs"))
    body = relayed if mesh.shape["rhs"] == 2 * LINE else local
    return jax.shard_map(body, mesh=mesh, in_specs=in_specs, out_specs=out_specs, check_vma=False)
```

```python
import functools
import jax
import jax.numpy as jnp
from jax import lax
from jax.experimental import pallas as pl
from jax.experimental.pallas import tpu as pltpu
from jax.sharding import PartitionSpec as P

LEAF = 24


def spread(shard, axis, root):
    mine = lax.axis_index(axis) == root
    return lax.psum(jnp.where(mine, shard, jnp.zeros_like(shard)), axis)


def local(local_rhs, top_rhs, diag_inv, top_inv, off_blocks, top_factor, targets):
    sub_count = local_rhs.shape[0]
    panel_width = local_rhs.shape[1]
    columns = local_rhs.shape[2]
    top_count = lax.axis_size("row")
    cand_count = sub_count + top_count
    acc_local = jnp.zeros((sub_count, panel_width, columns), jnp.float32)
    acc_top = jnp.zeros((top_count, panel_width, columns), jnp.float32)
    level_ranges = ((0, LEAF), (LEAF, LEAF + LEAF // 2), (LEAF + LEAF // 2, sub_count))
    solved = []
    for first_row, end_row in level_ranges:
        residual_rows = (
            local_rhs[first_row:end_row].astype(jnp.float32) - acc_local[first_row:end_row]
        ).astype(jnp.bfloat16)

        def apply_inverse(slice_part, offset, residual_rows=residual_rows):
            return jnp.einsum(
                "jxm,jme->jxe", slice_part, residual_rows, preferred_element_type=jnp.float32
            )

        level_partial = apply_inverse(
            lax.all_gather(diag_inv[first_row:end_row], "rhs", axis=1, tiled=True), jnp.int32(0)
        ).astype(jnp.bfloat16)
        solved.append(level_partial)
        target_codes = targets[first_row:end_row].reshape(-1)
        later_count = cand_count - end_row
        selector = (
            jnp.arange(later_count, dtype=jnp.int32)[:, None] == target_codes[None, :] - end_row
        ).astype(jnp.float32)

        def spread_updates(slice_part, offset, level_partial=level_partial, selector=selector):
            products = jnp.einsum(
                "yiko,yoq->yikq", slice_part, level_partial, preferred_element_type=jnp.float32
            )
            flattened = products.reshape(selector.shape[1], slice_part.shape[2], columns)
            return jnp.einsum("cn,nar->car", selector, flattened, precision=lax.Precision.HIGHEST)

        contrib = spread_updates(
            lax.all_gather(off_blocks[first_row:end_row], "rhs", axis=2, tiled=True), jnp.int32(0)
        )
        acc_local = acc_local.at[end_row:].add(contrib[: sub_count - end_row])
        acc_top = acc_top + contrib[sub_count - end_row :]
    inverse_rows = top_inv.reshape(1, 1, top_inv.shape[1], panel_width)
    top_full, inv_full = (
        lax.all_gather(top_factor, "rhs", axis=2, tiled=True),
        lax.all_gather(inverse_rows, "rhs", axis=2, tiled=True),
    )
    position = lax.axis_index("row")
    own_sum = lax.psum_scatter(
        acc_top.astype(jnp.bfloat16), "row", scatter_dimension=0, tiled=True
    ).astype(jnp.float32)
    base_value = top_rhs[0].astype(jnp.float32) - own_sum[0]

    def top_step(step_index, carry):
        carried, own_solution = carry
        residual_rows = (base_value - carried).astype(jnp.bfloat16)
        candidate = jnp.dot(
            inv_full[0, 0], residual_rows, preferred_element_type=jnp.float32
        ).astype(jnp.bfloat16)
        solution = spread(candidate, "row", step_index)
        own_solution = jnp.where(position == step_index, solution, own_solution)
        coupling_matrix = lax.dynamic_index_in_dim(top_full[0], step_index, 0, keepdims=False)
        update = jnp.dot(coupling_matrix, solution, preferred_element_type=jnp.float32)
        carried = carried + jnp.where(step_index < position, update, 0.0)
        return (carried, own_solution)

    initial_state = (
        jnp.zeros((panel_width, columns), jnp.float32),
        jnp.zeros((panel_width, columns), jnp.bfloat16),
    )
    own_separator = lax.fori_loop(0, top_count, top_step, initial_state)[1][None]
    return (jnp.concatenate(solved, axis=0), own_separator)


CHUNK = 2
LINE = 4
HOP = 2
READY = HOP * (LINE - 1) + 1
LEFT, RIGHT, ACROSS = 0, 1, 2
MESH = pl.DeviceIdType.MESH


def detour(k):
    return lax.rem(k, 6) == 3


def relay_kernel(
    rows, rhs_hbm, top_rhs_hbm, diag_hbm, top_inv_hbm, off_hbm, top_factor_hbm, targets,
    out_hbm, top_out_hbm,
    held, held_top, rhs, top_rhs, sol, acc, prod, part, parts, top_sol,
    load_sem, out_sem, send_sem, recv_sem, row_send, row_recv,
):
    sub, width, columns = rhs.shape
    chunks = 1 + sub // CHUNK
    cand = sub + rows
    row, me = lax.axis_index("row"), lax.axis_index("rhs")
    z, y = me // 2, lax.rem(me, 2)
    targets_of = {LEFT: me - 2, RIGHT: me + 2, ACROSS: z * 2 + 1 - y}
    peers = [lax.rem(row + p, rows) for p in range(1, rows)]

    def load(index, src, dst):
        return pltpu.make_async_copy(src, dst, load_sem.at[index])

    early, late = pl.ds(0, CHUNK), pl.ds(CHUNK, sub - CHUNK)
    first_loads = [
        load(0, top_inv_hbm.at[0], held_top.at[row, me, 0]),
        load(1, top_factor_hbm.at[0], held_top.at[row, me, pl.ds(1, 4)]),
        load(2, diag_hbm.at[early], held.at[me, early, 0]),
        load(3, off_hbm.at[early], held.at[me, early, pl.ds(1, 4)]),
        load(4, top_rhs_hbm.at[0], top_rhs.at[row]),
    ]
    next_loads = [
        load(5, diag_hbm.at[late], held.at[me, late, 0]),
        load(6, off_hbm.at[late], held.at[me, late, pl.ds(1, 4)]),
    ]
    rhs_load = load(7, rhs_hbm, rhs)

    barrier = pltpu.get_barrier_semaphore()
    for peer in peers:
        pl.semaphore_signal(barrier, inc=1, device_id=(peer, me), device_id_type=MESH)
    pl.semaphore_signal(barrier, inc=1, device_id=(row, targets_of[ACROSS]), device_id_type=MESH)

    @pl.when(z > 0)
    def _():
        pl.semaphore_signal(barrier, inc=1, device_id=(row, targets_of[LEFT]), device_id_type=MESH)

    @pl.when(z < LINE - 1)
    def _():
        pl.semaphore_signal(barrier, inc=1, device_id=(row, targets_of[RIGHT]), device_id_type=MESH)

    for copy in first_loads + next_loads + [rhs_load]:
        copy.start()

    def clear(c, carry):
        acc[c] = jnp.zeros((width, columns), jnp.float32)
        return carry

    lax.fori_loop(0, cand, clear, 0)
    for u in range(CHUNK):
        prod[u * 5 + 4] = jnp.zeros((width, columns), jnp.float32)

    ends = jnp.where(z == 0, 1, 0) + jnp.where(z == LINE - 1, 1, 0)
    pl.semaphore_wait(barrier, rows + 2 - ends)
    for copy in first_loads:
        copy.wait()

    def row_copy(kind, p, src, dst):
        return pltpu.make_async_remote_copy(
            src_ref=src, dst_ref=dst, send_sem=row_send.at[kind, p], recv_sem=row_recv.at[kind, row],
            device_id=(peers[p], me), device_id_type=MESH,
        )

    def row_arrival(kind, p, dst):
        return pltpu.make_async_remote_copy(
            src_ref=dst, dst_ref=dst, send_sem=row_send.at[kind, p], recv_sem=row_recv.at[kind, peers[p]],
            device_id=(peers[p], me), device_id_type=MESH,
        )

    for p in range(rows - 1):
        row_copy(0, p, top_rhs.at[row], top_rhs.at[row]).start()

    def either(k, src, count, act):
        @pl.when(k == 0)
        def _():
            act(held_top.at[row, pl.ds(src, count)])

        @pl.when(k > 0)
        def _():
            act(held.at[pl.ds(src, count), pl.ds((k - 1) * CHUNK, CHUNK)])

    def describe(ref, k, src, way):
        return pltpu.make_async_remote_copy(
            src_ref=ref, dst_ref=ref, send_sem=send_sem.at[way, k], recv_sem=recv_sem.at[k, src],
            device_id=(row, targets_of[way]), device_id_type=MESH,
        )

    def relay(k, src, wait, ways):
        def act(ref):
            if wait:
                describe(ref, k, src, ACROSS).wait_recv()
            for way, wanted in ways:
                @pl.when(wanted)
                def _(way=way):
                    describe(ref, k, src, way).start()

        either(k, src, 1, act)

    def drain(k):
        around = detour(k)
        sends = {
            LEFT: jnp.where(z > 0, (LINE - z) * jnp.where(around, 2, 1), 0),
            RIGHT: jnp.where(z < LINE - 1, (z + 1) * jnp.where(around, 2, 1), 0),
            ACROSS: jnp.where(around, 1, LINE),
        }
        for way, sizes in ((LEFT, (1, 2, 3, 4, 6)), (RIGHT, (1, 2, 3, 4, 6)), (ACROSS, (1, LINE))):
            for size in sizes:
                @pl.when(sends[way] == size)
                def _(way=way, size=size):
                    either(k, 0, size, lambda ref: describe(ref, k, 0, way).wait_send())

    def solve(k):
        first = (k - 1) * CHUNK
        half = LEAF + LEAF // 2
        codes = [[targets[first + u, j] for j in range(4)] for u in range(CHUNK)]
        for u in range(CHUNK):
            s = first + u
            residual = (rhs[s].astype(jnp.float32) - acc[s]).astype(jnp.bfloat16)
            inverse = held[:, s, 0].reshape(width, width)
            x = jnp.dot(inverse, residual, preferred_element_type=jnp.float32).astype(jnp.bfloat16)
            sol[s] = x
            blocks = jnp.concatenate([held[:, s, 1 + j].reshape(width, width) for j in range(4)], axis=0)
            prod[pl.ds(u * 5, 4)] = jnp.dot(blocks, x, preferred_element_type=jnp.float32).reshape(4, width, columns)
        pltpu.make_async_copy(sol.at[pl.ds(first, CHUNK)], out_hbm.at[pl.ds(first, CHUNK)], out_sem.at[0]).start()

        def add(c, carry):
            total = acc[c]
            for u in range(CHUNK):
                slot = jnp.int32(u * 5 + 4)
                for j in range(4):
                    slot = jnp.where(codes[u][j] == c, u * 5 + j, slot)
                total = total + prod[slot]
            acc[c] = total
            return carry

        lax.fori_loop(jnp.where(first < LEAF, LEAF, jnp.where(first < half, half, sub)), cand, add, 0)

    def step(i, carry):
        for d in range(LINE):
            k = i - HOP * d

            @pl.when((k >= 0) & (k < chunks))
            def _(k=k, d=d):
                straight = jnp.logical_not(detour(k))
                if d == 0:
                    @pl.when(k == 2)
                    def _():
                        for copy in next_loads:
                            copy.wait()

                    relay(k, me, False, ((LEFT, z > 0), (RIGHT, z < LINE - 1), (ACROSS, z >= 0)))
                else:
                    @pl.when(z >= d)
                    def _():
                        relay(k, me - 2 * d, True, ((RIGHT, z < LINE - 1), (ACROSS, straight)))

                    @pl.when(z + d < LINE)
                    def _():
                        relay(k, me + 2 * d, True, ((LEFT, z > 0), (ACROSS, straight)))

            k = i - HOP * d - 1

            @pl.when((k >= 0) & (k < chunks) & detour(k))
            def _(k=k, d=d):
                far = targets_of[ACROSS]
                if d == 0:
                    relay(k, far, True, ((LEFT, z > 0), (RIGHT, z < LINE - 1)))
                else:
                    @pl.when(z >= d)
                    def _():
                        relay(k, far - 2 * d, True, ((RIGHT, z < LINE - 1),))

                    @pl.when(z + d < LINE)
                    def _():
                        relay(k, far + 2 * d, True, ((LEFT, z > 0),))

        k = i - READY

        @pl.when(k >= 0)
        def _():
            @pl.when(jnp.logical_not(detour(k)))
            def _():
                for other in range(LINE):
                    relay(k, other * 2 + 1 - y, True, ())

            @pl.when(k == 0)
            def _():
                rhs_load.wait()
                for p in range(rows - 1):
                    row_copy(1, p, held_top.at[row], held_top.at[row]).start()

            @pl.when(k > 0)
            def _():
                solve(k)

        @pl.when(i > READY)
        def _():
            drain(i - READY - 1)

        return carry

    steps = chunks + READY
    lax.fori_loop(0, steps, step, 0)

    part[...] = acc[pl.ds(sub, rows)].astype(jnp.bfloat16)
    for p in range(rows - 1):
        row_copy(2, p, part, parts.at[row]).start()

    def drain_rest(k, carry):
        drain(k)
        return carry

    lax.fori_loop(chunks - 1, chunks, drain_rest, 0)
    for p in range(rows - 1):
        row_copy(0, p, top_rhs.at[row], top_rhs.at[row]).wait_send()
        row_copy(1, p, held_top.at[row], held_top.at[row]).wait_send()
        row_arrival(0, p, top_rhs.at[peers[p]]).wait_recv()
        row_arrival(1, p, held_top.at[peers[p]]).wait_recv()
    pltpu.make_async_copy(sol, out_hbm, out_sem.at[0]).wait()
    for p in range(rows - 1):
        row_arrival(2, p, parts.at[peers[p]]).wait_recv()

    for t in range(rows):
        base = acc[sub + t]
        for p in range(rows - 1):
            base = base + parts[peers[p], t].astype(jnp.float32)
        base = top_rhs[t].astype(jnp.float32) - base
        for earlier in range(t):
            factor = held_top[t, :, 1 + earlier].reshape(width, width)
            base = base - jnp.dot(factor, top_sol[earlier], preferred_element_type=jnp.float32)
        inverse = held_top[t, :, 0].reshape(width, width)
        top_sol[t] = jnp.dot(inverse, base.astype(jnp.bfloat16), preferred_element_type=jnp.float32).astype(jnp.bfloat16)
    last = pltpu.make_async_copy(top_sol.at[row], top_out_hbm.at[0], out_sem.at[1])
    last.start()
    for p in range(rows - 1):
        row_copy(2, p, part, parts.at[row]).wait_send()
    last.wait()


def relayed(local_rhs, top_rhs, diag_inv, top_inv, off_blocks, top_factor, targets):
    rows, ranks = lax.axis_size("row"), lax.axis_size("rhs")
    sub, width, columns = local_rhs.shape
    share = diag_inv.shape[1]
    chunks = 1 + sub // CHUNK
    bf16, f32 = jnp.bfloat16, jnp.float32
    return pl.pallas_call(
        functools.partial(relay_kernel, rows),
        out_shape=(
            jax.ShapeDtypeStruct(local_rhs.shape, bf16),
            jax.ShapeDtypeStruct(top_rhs.shape, bf16),
        ),
        in_specs=[pl.BlockSpec(memory_space=pltpu.HBM)] * 6 + [pl.BlockSpec(memory_space=pltpu.SMEM)],
        out_specs=(pl.BlockSpec(memory_space=pl.ANY),) * 2,
        scratch_shapes=[
            pltpu.VMEM((ranks, sub, 5, share, width), bf16),
            pltpu.VMEM((rows, ranks, 5, share, width), bf16),
            pltpu.VMEM((sub, width, columns), bf16),
            pltpu.VMEM((rows, width, columns), bf16),
            pltpu.VMEM((sub, width, columns), bf16),
            pltpu.VMEM((sub + rows, width, columns), f32),
            pltpu.VMEM((5 * CHUNK, width, columns), f32),
            pltpu.VMEM((rows, width, columns), bf16),
            pltpu.VMEM((rows, rows, width, columns), bf16),
            pltpu.VMEM((rows, width, columns), bf16),
            pltpu.SemaphoreType.DMA((8,)),
            pltpu.SemaphoreType.DMA((2,)),
            pltpu.SemaphoreType.DMA((3, chunks)),
            pltpu.SemaphoreType.DMA((chunks, ranks)),
            pltpu.SemaphoreType.DMA((3, rows - 1)),
            pltpu.SemaphoreType.DMA((3, rows)),
        ],
        compiler_params=pltpu.CompilerParams(
            collective_id=0, has_side_effects=True, vmem_limit_bytes=60 * 1024 * 1024
        ),
        cost_estimate=pl.CostEstimate(
            flops=10 * sub * width * width * columns, bytes_accessed=4 * local_rhs.size + 2 * off_blocks.size, transcendentals=0
        ),
    )(local_rhs, top_rhs, diag_inv, top_inv, off_blocks, top_factor, targets)


def solution(mesh):
    in_specs = (
        P("row", None, "rhs"),
        P("row", None, "rhs"),
        P("row", "rhs", None),
        P("row", "rhs", None),
        P("row", None, "rhs", None),
        P("row", None, "rhs", None),
        P("row", None),
    )
    out_specs = (P("row", None, "rhs"), P("row", None, "rhs"))
    body = relayed if mesh.shape["rhs"] == 2 * LINE else local
    return jax.shard_map(body, mesh=mesh, in_specs=in_specs, out_specs=out_specs, check_vma=False)
```

```python
import functools
import jax
import jax.numpy as jnp
from jax import lax
from jax.experimental import pallas as pl
from jax.experimental.pallas import tpu as pltpu
from jax.sharding import PartitionSpec as P

LEAF = 24


def spread(shard, axis, root):
    mine = lax.axis_index(axis) == root
    return lax.psum(jnp.where(mine, shard, jnp.zeros_like(shard)), axis)


def local(local_rhs, top_rhs, diag_inv, top_inv, off_blocks, top_factor, targets):
    sub_count = local_rhs.shape[0]
    panel_width = local_rhs.shape[1]
    columns = local_rhs.shape[2]
    top_count = lax.axis_size("row")
    cand_count = sub_count + top_count
    acc_local = jnp.zeros((sub_count, panel_width, columns), jnp.float32)
    acc_top = jnp.zeros((top_count, panel_width, columns), jnp.float32)
    level_ranges = ((0, LEAF), (LEAF, LEAF + LEAF // 2), (LEAF + LEAF // 2, sub_count))
    solved = []
    for first_row, end_row in level_ranges:
        residual_rows = (
            local_rhs[first_row:end_row].astype(jnp.float32) - acc_local[first_row:end_row]
        ).astype(jnp.bfloat16)

        def apply_inverse(slice_part, offset, residual_rows=residual_rows):
            return jnp.einsum(
                "jxm,jme->jxe", slice_part, residual_rows, preferred_element_type=jnp.float32
            )

        level_partial = apply_inverse(
            lax.all_gather(diag_inv[first_row:end_row], "rhs", axis=1, tiled=True), jnp.int32(0)
        ).astype(jnp.bfloat16)
        solved.append(level_partial)
        target_codes = targets[first_row:end_row].reshape(-1)
        later_count = cand_count - end_row
        selector = (
            jnp.arange(later_count, dtype=jnp.int32)[:, None] == target_codes[None, :] - end_row
        ).astype(jnp.float32)

        def spread_updates(slice_part, offset, level_partial=level_partial, selector=selector):
            products = jnp.einsum(
                "yiko,yoq->yikq", slice_part, level_partial, preferred_element_type=jnp.float32
            )
            flattened = products.reshape(selector.shape[1], slice_part.shape[2], columns)
            return jnp.einsum("cn,nar->car", selector, flattened, precision=lax.Precision.HIGHEST)

        contrib = spread_updates(
            lax.all_gather(off_blocks[first_row:end_row], "rhs", axis=2, tiled=True), jnp.int32(0)
        )
        acc_local = acc_local.at[end_row:].add(contrib[: sub_count - end_row])
        acc_top = acc_top + contrib[sub_count - end_row :]
    inverse_rows = top_inv.reshape(1, 1, top_inv.shape[1], panel_width)
    top_full, inv_full = (
        lax.all_gather(top_factor, "rhs", axis=2, tiled=True),
        lax.all_gather(inverse_rows, "rhs", axis=2, tiled=True),
    )
    position = lax.axis_index("row")
    own_sum = lax.psum_scatter(
        acc_top.astype(jnp.bfloat16), "row", scatter_dimension=0, tiled=True
    ).astype(jnp.float32)
    base_value = top_rhs[0].astype(jnp.float32) - own_sum[0]

    def top_step(step_index, carry):
        carried, own_solution = carry
        residual_rows = (base_value - carried).astype(jnp.bfloat16)
        candidate = jnp.dot(
            inv_full[0, 0], residual_rows, preferred_element_type=jnp.float32
        ).astype(jnp.bfloat16)
        solution = spread(candidate, "row", step_index)
        own_solution = jnp.where(position == step_index, solution, own_solution)
        coupling_matrix = lax.dynamic_index_in_dim(top_full[0], step_index, 0, keepdims=False)
        update = jnp.dot(coupling_matrix, solution, preferred_element_type=jnp.float32)
        carried = carried + jnp.where(step_index < position, update, 0.0)
        return (carried, own_solution)

    initial_state = (
        jnp.zeros((panel_width, columns), jnp.float32),
        jnp.zeros((panel_width, columns), jnp.bfloat16),
    )
    own_separator = lax.fori_loop(0, top_count, top_step, initial_state)[1][None]
    return (jnp.concatenate(solved, axis=0), own_separator)


CHUNK = 3
LINE = 4
HOP = 1
READY = HOP * (LINE - 1) + 1
LEFT, RIGHT, ACROSS = 0, 1, 2
MESH = pl.DeviceIdType.MESH


def detour(k):
    return k == 7


def relay_kernel(
    rows, rhs_hbm, top_rhs_hbm, diag_hbm, top_inv_hbm, off_hbm, top_factor_hbm, targets,
    out_hbm, top_out_hbm,
    held, held_top, rhs, top_rhs, sol, acc, prod, part, parts, top_sol,
    load_sem, out_sem, send_sem, recv_sem, row_send, row_recv,
):
    sub, width, columns = rhs.shape
    chunks = 1 + sub // CHUNK
    cand = sub + rows
    row, me = lax.axis_index("row"), lax.axis_index("rhs")
    z, y = me // 2, lax.rem(me, 2)
    targets_of = {LEFT: me - 2, RIGHT: me + 2, ACROSS: z * 2 + 1 - y}
    peers = [lax.rem(row + p, rows) for p in range(1, rows)]

    def load(index, src, dst):
        return pltpu.make_async_copy(src, dst, load_sem.at[index])

    early, late = pl.ds(0, CHUNK), pl.ds(CHUNK, sub - CHUNK)
    first_loads = [
        load(0, top_inv_hbm.at[0], held_top.at[row, me, 0]),
        load(1, top_factor_hbm.at[0], held_top.at[row, me, pl.ds(1, 4)]),
        load(2, diag_hbm.at[early], held.at[me, early, 0]),
        load(3, off_hbm.at[early], held.at[me, early, pl.ds(1, 4)]),
        load(4, top_rhs_hbm.at[0], top_rhs.at[row]),
    ]
    next_loads = [
        load(5, diag_hbm.at[late], held.at[me, late, 0]),
        load(6, off_hbm.at[late], held.at[me, late, pl.ds(1, 4)]),
    ]
    rhs_load = load(7, rhs_hbm, rhs)

    barrier = pltpu.get_barrier_semaphore()
    for peer in peers:
        pl.semaphore_signal(barrier, inc=1, device_id=(peer, me), device_id_type=MESH)
    pl.semaphore_signal(barrier, inc=1, device_id=(row, targets_of[ACROSS]), device_id_type=MESH)

    @pl.when(z > 0)
    def _():
        pl.semaphore_signal(barrier, inc=1, device_id=(row, targets_of[LEFT]), device_id_type=MESH)

    @pl.when(z < LINE - 1)
    def _():
        pl.semaphore_signal(barrier, inc=1, device_id=(row, targets_of[RIGHT]), device_id_type=MESH)

    for copy in first_loads + next_loads + [rhs_load]:
        copy.start()

    def clear(c, carry):
        acc[c] = jnp.zeros((width, columns), jnp.float32)
        return carry

    lax.fori_loop(0, cand, clear, 0)
    for u in range(CHUNK):
        prod[u * 5 + 4] = jnp.zeros((width, columns), jnp.float32)

    ends = jnp.where(z == 0, 1, 0) + jnp.where(z == LINE - 1, 1, 0)
    pl.semaphore_wait(barrier, rows + 2 - ends)
    for copy in first_loads:
        copy.wait()

    def row_copy(kind, p, src, dst):
        return pltpu.make_async_remote_copy(
            src_ref=src, dst_ref=dst, send_sem=row_send.at[kind, p], recv_sem=row_recv.at[kind, row],
            device_id=(peers[p], me), device_id_type=MESH,
        )

    def row_arrival(kind, p, dst):
        return pltpu.make_async_remote_copy(
            src_ref=dst, dst_ref=dst, send_sem=row_send.at[kind, p], recv_sem=row_recv.at[kind, peers[p]],
            device_id=(peers[p], me), device_id_type=MESH,
        )

    for p in range(rows - 1):
        row_copy(0, p, top_rhs.at[row], top_rhs.at[row]).start()

    def either(k, src, count, act):
        @pl.when(k == 0)
        def _():
            act(held_top.at[row, pl.ds(src, count)])

        @pl.when(k > 0)
        def _():
            act(held.at[pl.ds(src, count), pl.ds((k - 1) * CHUNK, CHUNK)])

    def describe(ref, k, src, way):
        return pltpu.make_async_remote_copy(
            src_ref=ref, dst_ref=ref, send_sem=send_sem.at[way, k], recv_sem=recv_sem.at[k, src],
            device_id=(row, targets_of[way]), device_id_type=MESH,
        )

    def relay(k, src, wait, ways):
        def act(ref):
            if wait:
                describe(ref, k, src, ACROSS).wait_recv()
            for way, wanted in ways:
                @pl.when(wanted)
                def _(way=way):
                    describe(ref, k, src, way).start()

        either(k, src, 1, act)

    def drain(k):
        around = detour(k)
        sends = {
            LEFT: jnp.where(z > 0, (LINE - z) * jnp.where(around, 2, 1), 0),
            RIGHT: jnp.where(z < LINE - 1, (z + 1) * jnp.where(around, 2, 1), 0),
            ACROSS: jnp.where(around, 1, LINE),
        }
        for way, sizes in ((LEFT, (1, 2, 3, 4, 6)), (RIGHT, (1, 2, 3, 4, 6)), (ACROSS, (1, LINE))):
            for size in sizes:
                @pl.when(sends[way] == size)
                def _(way=way, size=size):
                    either(k, 0, size, lambda ref: describe(ref, k, 0, way).wait_send())

    def solve(k):
        first = (k - 1) * CHUNK
        half = LEAF + LEAF // 2
        codes = [[targets[j, first + u] for j in range(4)] for u in range(CHUNK)]
        residuals = [
            (rhs[first + u].astype(jnp.float32) - acc[first + u]).astype(jnp.bfloat16) for u in range(CHUNK)
        ]
        solved = [
            jnp.dot(held[:, first + u, 0].reshape(width, width), residuals[u], preferred_element_type=jnp.float32)
            for u in range(CHUNK)
        ]
        solved = [x.astype(jnp.bfloat16) for x in solved]
        for u in range(CHUNK):
            sol[first + u] = solved[u]
        for u in range(CHUNK):
            blocks = [held[:, first + u, 1 + j].reshape(width, width) for j in range(4)]
            updates = jnp.dot(jnp.concatenate(blocks, axis=0), solved[u], preferred_element_type=jnp.float32)
            prod[pl.ds(u * 5, 4)] = updates.reshape(4, width, columns)
        pltpu.make_async_copy(sol.at[pl.ds(first, CHUNK)], out_hbm.at[pl.ds(first, CHUNK)], out_sem.at[0]).start()

        least = jnp.where(first < LEAF, LEAF, jnp.where(first < half, half, sub))

        def add(pair, carry):
            for c in (least + 2 * pair, least + 2 * pair + 1):
                total = acc[c]
                for u in range(CHUNK):
                    slot = jnp.int32(u * 5 + 4)
                    for j in range(4):
                        slot = jnp.where(codes[u][j] == c, u * 5 + j, slot)
                    total = total + prod[slot]
                acc[c] = total
            return carry

        lax.fori_loop(0, (cand - least) // 2, add, 0)

    def step(i, carry):
        for d in range(LINE):
            k = i - HOP * d

            @pl.when((k >= 0) & (k < chunks))
            def _(k=k, d=d):
                straight = jnp.logical_not(detour(k))
                if d == 0:
                    @pl.when(k == 2)
                    def _():
                        for copy in next_loads:
                            copy.wait()

                    relay(k, me, False, ((LEFT, z > 0), (RIGHT, z < LINE - 1), (ACROSS, z >= 0)))
                else:
                    @pl.when(z >= d)
                    def _():
                        relay(k, me - 2 * d, True, ((RIGHT, z < LINE - 1), (ACROSS, straight)))

                    @pl.when(z + d < LINE)
                    def _():
                        relay(k, me + 2 * d, True, ((LEFT, z > 0), (ACROSS, straight)))

            k = i - HOP * d - 1

            @pl.when((k >= 0) & (k < chunks) & detour(k))
            def _(k=k, d=d):
                far = targets_of[ACROSS]
                if d == 0:
                    relay(k, far, True, ((LEFT, z > 0), (RIGHT, z < LINE - 1)))
                else:
                    @pl.when(z >= d)
                    def _():
                        relay(k, far - 2 * d, True, ((RIGHT, z < LINE - 1),))

                    @pl.when(z + d < LINE)
                    def _():
                        relay(k, far + 2 * d, True, ((LEFT, z > 0),))

        k = i - READY

        @pl.when(k >= 0)
        def _():
            @pl.when(jnp.logical_not(detour(k)))
            def _():
                for other in range(LINE):
                    relay(k, other * 2 + 1 - y, True, ())

            @pl.when(k == 0)
            def _():
                rhs_load.wait()
                for p in range(rows - 1):
                    row_copy(1, p, held_top.at[row], held_top.at[row]).start()

            @pl.when(k > 0)
            def _():
                solve(k)

        @pl.when(i > READY)
        def _():
            drain(i - READY - 1)

        return carry

    steps = chunks + READY
    lax.fori_loop(0, steps, step, 0)

    part[...] = acc[pl.ds(sub, rows)].astype(jnp.bfloat16)
    for p in range(rows - 1):
        row_copy(2, p, part, parts.at[row]).start()

    def drain_rest(k, carry):
        drain(k)
        return carry

    lax.fori_loop(chunks - 1, chunks, drain_rest, 0)
    for p in range(rows - 1):
        row_copy(0, p, top_rhs.at[row], top_rhs.at[row]).wait_send()
        row_copy(1, p, held_top.at[row], held_top.at[row]).wait_send()
        row_arrival(0, p, top_rhs.at[peers[p]]).wait_recv()
        row_arrival(1, p, held_top.at[peers[p]]).wait_recv()
    pltpu.make_async_copy(sol, out_hbm, out_sem.at[0]).wait()
    for p in range(rows - 1):
        row_arrival(2, p, parts.at[peers[p]]).wait_recv()

    for t in range(rows):
        base = acc[sub + t]
        for p in range(rows - 1):
            base = base + parts[peers[p], t].astype(jnp.float32)
        base = top_rhs[t].astype(jnp.float32) - base
        for earlier in range(t):
            factor = held_top[t, :, 1 + earlier].reshape(width, width)
            base = base - jnp.dot(factor, top_sol[earlier], preferred_element_type=jnp.float32)
        inverse = held_top[t, :, 0].reshape(width, width)
        top_sol[t] = jnp.dot(inverse, base.astype(jnp.bfloat16), preferred_element_type=jnp.float32).astype(jnp.bfloat16)
    last = pltpu.make_async_copy(top_sol.at[row], top_out_hbm.at[0], out_sem.at[1])
    last.start()
    for p in range(rows - 1):
        row_copy(2, p, part, parts.at[row]).wait_send()
    last.wait()


def place_kernel(local_in, top_in, local_out, top_out, sems):
    sub = local_in.shape[0]
    parts = [pl.ds(first, CHUNK) for first in range(0, sub, CHUNK)]
    copies = [
        pltpu.make_async_copy(local_in.at[part], local_out.at[part], sems.at[1 + index])
        for index, part in enumerate(parts)
    ]
    copies.append(pltpu.make_async_copy(top_in, top_out, sems.at[0]))
    for copy in copies:
        copy.start()
    for copy in copies:
        copy.wait()


def placed(local_solution, top_solution):
    pieces = local_solution.shape[0] // CHUNK
    return pl.pallas_call(
        place_kernel,
        out_shape=tuple(jax.ShapeDtypeStruct(x.shape, x.dtype) for x in (local_solution, top_solution)),
        in_specs=[pl.BlockSpec(memory_space=pl.ANY)] * 2,
        out_specs=(pl.BlockSpec(memory_space=pl.ANY),) * 2,
        scratch_shapes=[pltpu.SemaphoreType.DMA((1 + pieces,))],
    )(local_solution, top_solution)


def relayed(local_rhs, top_rhs, diag_inv, top_inv, off_blocks, top_factor, targets):
    rows, ranks = lax.axis_size("row"), lax.axis_size("rhs")
    sub, width, columns = local_rhs.shape
    share = diag_inv.shape[1]
    chunks = 1 + sub // CHUNK
    bf16, f32 = jnp.bfloat16, jnp.float32
    solutions = pl.pallas_call(
        functools.partial(relay_kernel, rows),
        out_shape=(
            jax.ShapeDtypeStruct(local_rhs.shape, bf16),
            jax.ShapeDtypeStruct(top_rhs.shape, bf16),
        ),
        in_specs=[pl.BlockSpec(memory_space=pltpu.HBM)] * 6 + [pl.BlockSpec(memory_space=pltpu.SMEM)],
        out_specs=(pl.BlockSpec(memory_space=pl.ANY),) * 2,
        scratch_shapes=[
            pltpu.VMEM((ranks, sub, 5, share, width), bf16),
            pltpu.VMEM((rows, ranks, 5, share, width), bf16),
            pltpu.VMEM((sub, width, columns), bf16),
            pltpu.VMEM((rows, width, columns), bf16),
            pltpu.VMEM((sub, width, columns), bf16),
            pltpu.VMEM((sub + rows, width, columns), f32),
            pltpu.VMEM((5 * CHUNK, width, columns), f32),
            pltpu.VMEM((rows, width, columns), bf16),
            pltpu.VMEM((rows, rows, width, columns), bf16),
            pltpu.VMEM((rows, width, columns), bf16),
            pltpu.SemaphoreType.DMA((8,)),
            pltpu.SemaphoreType.DMA((2,)),
            pltpu.SemaphoreType.DMA((3, chunks)),
            pltpu.SemaphoreType.DMA((chunks, ranks)),
            pltpu.SemaphoreType.DMA((3, rows - 1)),
            pltpu.SemaphoreType.DMA((3, rows)),
        ],
        compiler_params=pltpu.CompilerParams(
            collective_id=0, has_side_effects=True, vmem_limit_bytes=60 * 1024 * 1024
        ),
        cost_estimate=pl.CostEstimate(
            flops=10 * sub * width * width * columns, bytes_accessed=4 * local_rhs.size + 2 * off_blocks.size, transcendentals=0
        ),
    )(local_rhs, top_rhs, diag_inv, top_inv, off_blocks, top_factor, targets.T)
    return placed(*solutions)


def solution(mesh):
    in_specs = (
        P("row", None, "rhs"),
        P("row", None, "rhs"),
        P("row", "rhs", None),
        P("row", "rhs", None),
        P("row", None, "rhs", None),
        P("row", None, "rhs", None),
        P("row", None),
    )
    out_specs = (P("row", None, "rhs"), P("row", None, "rhs"))
    body = relayed if mesh.shape["rhs"] == 2 * LINE else local
    return jax.shard_map(body, mesh=mesh, in_specs=in_specs, out_specs=out_specs, check_vma=False)
```

```python
import functools
import jax
import jax.numpy as jnp
from jax import lax
from jax.experimental import pallas as pl
from jax.experimental.pallas import tpu as pltpu
from jax.sharding import PartitionSpec as P

LEAF = 24


def spread(shard, axis, root):
    mine = lax.axis_index(axis) == root
    return lax.psum(jnp.where(mine, shard, jnp.zeros_like(shard)), axis)


def local(local_rhs, top_rhs, diag_inv, top_inv, off_blocks, top_factor, targets):
    sub_count = local_rhs.shape[0]
    panel_width = local_rhs.shape[1]
    columns = local_rhs.shape[2]
    top_count = lax.axis_size("row")
    cand_count = sub_count + top_count
    acc_local = jnp.zeros((sub_count, panel_width, columns), jnp.float32)
    acc_top = jnp.zeros((top_count, panel_width, columns), jnp.float32)
    level_ranges = ((0, LEAF), (LEAF, LEAF + LEAF // 2), (LEAF + LEAF // 2, sub_count))
    solved = []
    for first_row, end_row in level_ranges:
        residual_rows = (
            local_rhs[first_row:end_row].astype(jnp.float32) - acc_local[first_row:end_row]
        ).astype(jnp.bfloat16)

        def apply_inverse(slice_part, offset, residual_rows=residual_rows):
            return jnp.einsum(
                "jxm,jme->jxe", slice_part, residual_rows, preferred_element_type=jnp.float32
            )

        level_partial = apply_inverse(
            lax.all_gather(diag_inv[first_row:end_row], "rhs", axis=1, tiled=True), jnp.int32(0)
        ).astype(jnp.bfloat16)
        solved.append(level_partial)
        target_codes = targets[first_row:end_row].reshape(-1)
        later_count = cand_count - end_row
        selector = (
            jnp.arange(later_count, dtype=jnp.int32)[:, None] == target_codes[None, :] - end_row
        ).astype(jnp.float32)

        def spread_updates(slice_part, offset, level_partial=level_partial, selector=selector):
            products = jnp.einsum(
                "yiko,yoq->yikq", slice_part, level_partial, preferred_element_type=jnp.float32
            )
            flattened = products.reshape(selector.shape[1], slice_part.shape[2], columns)
            return jnp.einsum("cn,nar->car", selector, flattened, precision=lax.Precision.HIGHEST)

        contrib = spread_updates(
            lax.all_gather(off_blocks[first_row:end_row], "rhs", axis=2, tiled=True), jnp.int32(0)
        )
        acc_local = acc_local.at[end_row:].add(contrib[: sub_count - end_row])
        acc_top = acc_top + contrib[sub_count - end_row :]
    inverse_rows = top_inv.reshape(1, 1, top_inv.shape[1], panel_width)
    top_full, inv_full = (
        lax.all_gather(top_factor, "rhs", axis=2, tiled=True),
        lax.all_gather(inverse_rows, "rhs", axis=2, tiled=True),
    )
    position = lax.axis_index("row")
    own_sum = lax.psum_scatter(
        acc_top.astype(jnp.bfloat16), "row", scatter_dimension=0, tiled=True
    ).astype(jnp.float32)
    base_value = top_rhs[0].astype(jnp.float32) - own_sum[0]

    def top_step(step_index, carry):
        carried, own_solution = carry
        residual_rows = (base_value - carried).astype(jnp.bfloat16)
        candidate = jnp.dot(
            inv_full[0, 0], residual_rows, preferred_element_type=jnp.float32
        ).astype(jnp.bfloat16)
        solution = spread(candidate, "row", step_index)
        own_solution = jnp.where(position == step_index, solution, own_solution)
        coupling_matrix = lax.dynamic_index_in_dim(top_full[0], step_index, 0, keepdims=False)
        update = jnp.dot(coupling_matrix, solution, preferred_element_type=jnp.float32)
        carried = carried + jnp.where(step_index < position, update, 0.0)
        return (carried, own_solution)

    initial_state = (
        jnp.zeros((panel_width, columns), jnp.float32),
        jnp.zeros((panel_width, columns), jnp.bfloat16),
    )
    own_separator = lax.fori_loop(0, top_count, top_step, initial_state)[1][None]
    return (jnp.concatenate(solved, axis=0), own_separator)


CHUNK = 2
LINE = 4
HOP = 2
READY = HOP * (LINE - 1) + 1
LEFT, RIGHT, ACROSS = 0, 1, 2
MESH = pl.DeviceIdType.MESH


def detour(k):
    return lax.rem(k, 6) == 3


def times_turned(left, right):
    return lax.dot_general(left, right, (((1,), (1,)), ((), ())), preferred_element_type=jnp.float32)


def relay_kernel(
    rows, rhs_hbm, top_rhs_hbm, diag_hbm, top_inv_hbm, off_hbm, top_factor_hbm, targets,
    out_hbm, top_out_hbm,
    held, held_top, rhs, top_rhs, sol, acc, prod, part, parts, top_sol,
    turned, top_rhs_turned, gathered, top_out,
    load_sem, out_sem, send_sem, recv_sem, row_send, row_recv, top_send, top_recv,
):
    sub, width, columns = rhs.shape
    chunks = 1 + sub // CHUNK
    cand = sub + rows
    share = columns // rows
    row, me = lax.axis_index("row"), lax.axis_index("rhs")
    z, y = me // 2, lax.rem(me, 2)
    targets_of = {LEFT: me - 2, RIGHT: me + 2, ACROSS: z * 2 + 1 - y}
    peers = [lax.rem(row + p, rows) for p in range(1, rows)]

    def load(index, src, dst):
        return pltpu.make_async_copy(src, dst, load_sem.at[index])

    early, late = pl.ds(0, CHUNK), pl.ds(CHUNK, sub - CHUNK)
    first_loads = [
        load(0, top_inv_hbm.at[0], held_top.at[row, me, 0]),
        load(1, top_factor_hbm.at[0], held_top.at[row, me, pl.ds(1, 4)]),
        load(2, diag_hbm.at[early], held.at[me, early, 0]),
        load(3, off_hbm.at[early], held.at[me, early, pl.ds(1, 4)]),
        load(4, top_rhs_hbm.at[0], top_rhs.at[row]),
    ]
    next_loads = [
        load(5, diag_hbm.at[late], held.at[me, late, 0]),
        load(6, off_hbm.at[late], held.at[me, late, pl.ds(1, 4)]),
    ]
    rhs_load = load(7, rhs_hbm, rhs)

    barrier = pltpu.get_barrier_semaphore()
    for peer in peers:
        pl.semaphore_signal(barrier, inc=1, device_id=(peer, me), device_id_type=MESH)
    pl.semaphore_signal(barrier, inc=1, device_id=(row, targets_of[ACROSS]), device_id_type=MESH)

    @pl.when(z > 0)
    def _():
        pl.semaphore_signal(barrier, inc=1, device_id=(row, targets_of[LEFT]), device_id_type=MESH)

    @pl.when(z < LINE - 1)
    def _():
        pl.semaphore_signal(barrier, inc=1, device_id=(row, targets_of[RIGHT]), device_id_type=MESH)

    for copy in first_loads + next_loads + [rhs_load]:
        copy.start()

    def clear(c, carry):
        acc[c] = jnp.zeros((width, columns), jnp.float32)
        return carry

    lax.fori_loop(0, cand, clear, 0)
    for u in range(CHUNK):
        prod[u * 5 + 4] = jnp.zeros((width, columns), jnp.float32)

    ends = jnp.where(z == 0, 1, 0) + jnp.where(z == LINE - 1, 1, 0)
    pl.semaphore_wait(barrier, rows + 2 - ends)
    for copy in first_loads:
        copy.wait()

    def row_copy(kind, p, src, dst):
        return pltpu.make_async_remote_copy(
            src_ref=src, dst_ref=dst, send_sem=row_send.at[kind, p], recv_sem=row_recv.at[kind, row],
            device_id=(peers[p], me), device_id_type=MESH,
        )

    def row_arrival(kind, p, dst):
        return pltpu.make_async_remote_copy(
            src_ref=dst, dst_ref=dst, send_sem=row_send.at[kind, p], recv_sem=row_recv.at[kind, peers[p]],
            device_id=(peers[p], me), device_id_type=MESH,
        )

    for p in range(rows - 1):
        row_copy(0, p, top_rhs.at[row], top_rhs.at[row]).start()

    def either(k, src, count, act):
        @pl.when(k == 0)
        def _():
            act(held_top.at[row, pl.ds(src, count)])

        @pl.when(k > 0)
        def _():
            act(held.at[pl.ds(src, count), pl.ds((k - 1) * CHUNK, CHUNK)])

    def describe(ref, k, src, way):
        return pltpu.make_async_remote_copy(
            src_ref=ref, dst_ref=ref, send_sem=send_sem.at[way, k], recv_sem=recv_sem.at[k, src],
            device_id=(row, targets_of[way]), device_id_type=MESH,
        )

    def relay(k, src, wait, ways):
        def act(ref):
            if wait:
                describe(ref, k, src, ACROSS).wait_recv()
            for way, wanted in ways:
                @pl.when(wanted)
                def _(way=way):
                    describe(ref, k, src, way).start()

        either(k, src, 1, act)

    def drain(k):
        around = detour(k)
        sends = {
            LEFT: jnp.where(z > 0, (LINE - z) * jnp.where(around, 2, 1), 0),
            RIGHT: jnp.where(z < LINE - 1, (z + 1) * jnp.where(around, 2, 1), 0),
            ACROSS: jnp.where(around, 1, LINE),
        }
        for way, sizes in ((LEFT, (1, 2, 3, 4, 6)), (RIGHT, (1, 2, 3, 4, 6)), (ACROSS, (1, LINE))):
            for size in sizes:
                @pl.when(sends[way] == size)
                def _(way=way, size=size):
                    either(k, 0, size, lambda ref: describe(ref, k, 0, way).wait_send())

    def solve(k):
        first = (k - 1) * CHUNK
        half = LEAF + LEAF // 2
        codes = [[targets[j, first + u] for j in range(4)] for u in range(CHUNK)]
        residuals = [
            (rhs[first + u].astype(jnp.float32) - acc[first + u]).astype(jnp.bfloat16) for u in range(CHUNK)
        ]
        solved = [
            jnp.dot(held[:, first + u, 0].reshape(width, width), residuals[u], preferred_element_type=jnp.float32)
            for u in range(CHUNK)
        ]
        solved = [x.astype(jnp.bfloat16) for x in solved]
        for u in range(CHUNK):
            sol[first + u] = solved[u]
        for u in range(CHUNK):
            blocks = [held[:, first + u, 1 + j].reshape(width, width) for j in range(4)]
            updates = jnp.dot(jnp.concatenate(blocks, axis=0), solved[u], preferred_element_type=jnp.float32)
            prod[pl.ds(u * 5, 4)] = updates.reshape(4, width, columns)
        pltpu.make_async_copy(sol.at[pl.ds(first, CHUNK)], out_hbm.at[pl.ds(first, CHUNK)], out_sem.at[0]).start()

        least = jnp.where(first < LEAF, LEAF, jnp.where(first < half, half, sub))

        def add(pair, carry):
            for c in (least + 2 * pair, least + 2 * pair + 1):
                total = acc[c]
                for u in range(CHUNK):
                    slot = jnp.int32(u * 5 + 4)
                    for j in range(4):
                        slot = jnp.where(codes[u][j] == c, u * 5 + j, slot)
                    total = total + prod[slot]
                acc[c] = total
            return carry

        lax.fori_loop(0, (cand - least) // 2, add, 0)

    def step(i, carry):
        for d in range(LINE):
            k = i - HOP * d

            @pl.when((k >= 0) & (k < chunks))
            def _(k=k, d=d):
                straight = jnp.logical_not(detour(k))
                if d == 0:
                    @pl.when(k == 2)
                    def _():
                        for copy in next_loads:
                            copy.wait()

                    relay(k, me, False, ((LEFT, z > 0), (RIGHT, z < LINE - 1), (ACROSS, z >= 0)))
                else:
                    @pl.when(z >= d)
                    def _():
                        relay(k, me - 2 * d, True, ((RIGHT, z < LINE - 1), (ACROSS, straight)))

                    @pl.when(z + d < LINE)
                    def _():
                        relay(k, me + 2 * d, True, ((LEFT, z > 0), (ACROSS, straight)))

            k = i - HOP * d - 1

            @pl.when((k >= 0) & (k < chunks) & detour(k))
            def _(k=k, d=d):
                far = targets_of[ACROSS]
                if d == 0:
                    relay(k, far, True, ((LEFT, z > 0), (RIGHT, z < LINE - 1)))
                else:
                    @pl.when(z >= d)
                    def _():
                        relay(k, far - 2 * d, True, ((RIGHT, z < LINE - 1),))

                    @pl.when(z + d < LINE)
                    def _():
                        relay(k, far + 2 * d, True, ((LEFT, z > 0),))

        k = i - READY

        @pl.when(k >= 0)
        def _():
            @pl.when(jnp.logical_not(detour(k)))
            def _():
                for other in range(LINE):
                    relay(k, other * 2 + 1 - y, True, ())

            @pl.when(k == 0)
            def _():
                rhs_load.wait()
                for p in range(rows - 1):
                    row_arrival(0, p, top_rhs.at[peers[p]]).wait_recv()
                for t in range(rows):
                    top_rhs_turned[t] = top_rhs[t].astype(jnp.float32).T
                for p in range(rows - 1):
                    row_copy(1, p, held_top.at[row], held_top.at[row]).start()

            @pl.when(k > 0)
            def _():
                solve(k)

        @pl.when(i > READY)
        def _():
            drain(i - READY - 1)

        return carry

    steps = chunks + READY
    lax.fori_loop(0, steps, step, 0)

    mine = pl.ds(pl.multiple_of(row * share, share), share)
    for t in range(rows):
        turned[t] = acc[sub + t].T
        part[t] = turned[t].astype(jnp.bfloat16)
    slices = [part.at[:, pl.ds(pl.multiple_of(peer * share, share), share)] for peer in peers]
    for p in range(rows - 1):
        row_copy(2, p, slices[p], parts.at[row]).start()

    def drain_rest(k, carry):
        drain(k)
        return carry

    lax.fori_loop(chunks - 1, chunks, drain_rest, 0)
    for p in range(rows - 1):
        row_copy(0, p, top_rhs.at[row], top_rhs.at[row]).wait_send()
        row_copy(1, p, held_top.at[row], held_top.at[row]).wait_send()
        row_arrival(1, p, held_top.at[peers[p]]).wait_recv()
    pltpu.make_async_copy(sol, out_hbm, out_sem.at[0]).wait()
    for p in range(rows - 1):
        row_arrival(2, p, parts.at[peers[p]]).wait_recv()

    def solved_copy(t):
        return pltpu.make_async_remote_copy(
            src_ref=top_sol.at[t], dst_ref=gathered.at[row], send_sem=top_send.at[t], recv_sem=top_recv.at[row],
            device_id=(t, me), device_id_type=MESH,
        )

    for t in range(rows):
        base = turned[t, mine]
        for p in range(rows - 1):
            base = base + parts[peers[p], t].astype(jnp.float32)
        base = top_rhs_turned[t, mine] - base
        for earlier in range(t):
            factor = held_top[t, :, 1 + earlier].reshape(width, width)
            base = base - times_turned(top_sol[earlier], factor)
        inverse = held_top[t, :, 0].reshape(width, width)
        top_sol[t] = times_turned(base.astype(jnp.bfloat16), inverse).astype(jnp.bfloat16)

        @pl.when(row != t)
        def _(t=t):
            solved_copy(t).start()

        @pl.when(row == t)
        def _(t=t):
            gathered[row] = top_sol[t]

    for p in range(rows - 1):
        pltpu.make_async_remote_copy(
            src_ref=top_sol.at[0], dst_ref=gathered.at[peers[p]], send_sem=top_send.at[0], recv_sem=top_recv.at[peers[p]],
            device_id=(peers[p], me), device_id_type=MESH,
        ).wait_recv()
    owned = gathered[...].reshape(columns, width).astype(jnp.float32)
    top_out[...] = owned.T.astype(jnp.bfloat16)
    last = pltpu.make_async_copy(top_out, top_out_hbm.at[0], out_sem.at[1])
    last.start()
    for p in range(rows - 1):
        row_copy(2, p, slices[p], parts.at[row]).wait_send()
    for t in range(rows):
        @pl.when(row != t)
        def _(t=t):
            solved_copy(t).wait_send()
    last.wait()


def place_kernel(local_in, top_in, local_out, top_out, sems):
    copies = [
        pltpu.make_async_copy(local_in, local_out, sems.at[0]),
        pltpu.make_async_copy(top_in, top_out, sems.at[1]),
    ]
    for copy in copies:
        copy.start()
    for copy in copies:
        copy.wait()


def placed(local_solution, top_solution):
    return pl.pallas_call(
        place_kernel,
        out_shape=tuple(jax.ShapeDtypeStruct(x.shape, x.dtype) for x in (local_solution, top_solution)),
        in_specs=[pl.BlockSpec(memory_space=pltpu.VMEM)] * 2,
        out_specs=(pl.BlockSpec(memory_space=pl.ANY),) * 2,
        scratch_shapes=[pltpu.SemaphoreType.DMA((2,))],
        compiler_params=pltpu.CompilerParams(vmem_limit_bytes=32 * 1024 * 1024),
    )(local_solution, top_solution)


def relayed(local_rhs, top_rhs, diag_inv, top_inv, off_blocks, top_factor, targets):
    rows, ranks = lax.axis_size("row"), lax.axis_size("rhs")
    sub, width, columns = local_rhs.shape
    share = diag_inv.shape[1]
    chunks = 1 + sub // CHUNK
    bf16, f32 = jnp.bfloat16, jnp.float32
    solutions = pl.pallas_call(
        functools.partial(relay_kernel, rows),
        out_shape=(
            jax.ShapeDtypeStruct(local_rhs.shape, bf16),
            jax.ShapeDtypeStruct(top_rhs.shape, bf16),
        ),
        in_specs=[pl.BlockSpec(memory_space=pltpu.HBM)] * 6 + [pl.BlockSpec(memory_space=pltpu.SMEM)],
        out_specs=(pl.BlockSpec(memory_space=pl.ANY),) * 2,
        scratch_shapes=[
            pltpu.VMEM((ranks, sub, 5, share, width), bf16),
            pltpu.VMEM((rows, ranks, 5, share, width), bf16),
            pltpu.VMEM((sub, width, columns), bf16),
            pltpu.VMEM((rows, width, columns), bf16),
            pltpu.VMEM((sub, width, columns), bf16),
            pltpu.VMEM((sub + rows, width, columns), f32),
            pltpu.VMEM((5 * CHUNK, width, columns), f32),
            pltpu.VMEM((rows, width, columns), bf16),
            pltpu.VMEM((rows, rows, columns // rows, width), bf16),
            pltpu.VMEM((rows, columns // rows, width), bf16),
            pltpu.VMEM((rows, columns, width), f32),
            pltpu.VMEM((rows, columns, width), f32),
            pltpu.VMEM((rows, columns // rows, width), bf16),
            pltpu.VMEM((width, columns), bf16),
            pltpu.SemaphoreType.DMA((8,)),
            pltpu.SemaphoreType.DMA((2,)),
            pltpu.SemaphoreType.DMA((3, chunks)),
            pltpu.SemaphoreType.DMA((chunks, ranks)),
            pltpu.SemaphoreType.DMA((3, rows - 1)),
            pltpu.SemaphoreType.DMA((3, rows)),
            pltpu.SemaphoreType.DMA((rows,)),
            pltpu.SemaphoreType.DMA((rows,)),
        ],
        compiler_params=pltpu.CompilerParams(
            collective_id=0, has_side_effects=True, vmem_limit_bytes=60 * 1024 * 1024
        ),
        cost_estimate=pl.CostEstimate(
            flops=10 * sub * width * width * columns, bytes_accessed=4 * local_rhs.size + 2 * off_blocks.size, transcendentals=0
        ),
    )(local_rhs, top_rhs, diag_inv, top_inv, off_blocks, top_factor, targets.T)
    return placed(*solutions)


def solution(mesh):
    in_specs = (
        P("row", None, "rhs"),
        P("row", None, "rhs"),
        P("row", "rhs", None),
        P("row", "rhs", None),
        P("row", None, "rhs", None),
        P("row", None, "rhs", None),
        P("row", None),
    )
    out_specs = (P("row", None, "rhs"), P("row", None, "rhs"))
    body = relayed if mesh.shape["rhs"] == 2 * LINE else local
    return jax.shard_map(body, mesh=mesh, in_specs=in_specs, out_specs=out_specs, check_vma=False)
```

```python
import functools
import jax
import jax.numpy as jnp
from jax import lax
from jax.experimental import pallas as pl
from jax.experimental.pallas import tpu as pltpu
from jax.sharding import PartitionSpec as P

LEAF = 24


def spread(shard, axis, root):
    mine = lax.axis_index(axis) == root
    return lax.psum(jnp.where(mine, shard, jnp.zeros_like(shard)), axis)


def local(local_rhs, top_rhs, diag_inv, top_inv, off_blocks, top_factor, targets):
    sub_count = local_rhs.shape[0]
    panel_width = local_rhs.shape[1]
    columns = local_rhs.shape[2]
    top_count = lax.axis_size("row")
    cand_count = sub_count + top_count
    acc_local = jnp.zeros((sub_count, panel_width, columns), jnp.float32)
    acc_top = jnp.zeros((top_count, panel_width, columns), jnp.float32)
    level_ranges = ((0, LEAF), (LEAF, LEAF + LEAF // 2), (LEAF + LEAF // 2, sub_count))
    solved = []
    for first_row, end_row in level_ranges:
        residual_rows = (
            local_rhs[first_row:end_row].astype(jnp.float32) - acc_local[first_row:end_row]
        ).astype(jnp.bfloat16)

        def apply_inverse(slice_part, offset, residual_rows=residual_rows):
            return jnp.einsum(
                "jxm,jme->jxe", slice_part, residual_rows, preferred_element_type=jnp.float32
            )

        level_partial = apply_inverse(
            lax.all_gather(diag_inv[first_row:end_row], "rhs", axis=1, tiled=True), jnp.int32(0)
        ).astype(jnp.bfloat16)
        solved.append(level_partial)
        target_codes = targets[first_row:end_row].reshape(-1)
        later_count = cand_count - end_row
        selector = (
            jnp.arange(later_count, dtype=jnp.int32)[:, None] == target_codes[None, :] - end_row
        ).astype(jnp.float32)

        def spread_updates(slice_part, offset, level_partial=level_partial, selector=selector):
            products = jnp.einsum(
                "yiko,yoq->yikq", slice_part, level_partial, preferred_element_type=jnp.float32
            )
            flattened = products.reshape(selector.shape[1], slice_part.shape[2], columns)
            return jnp.einsum("cn,nar->car", selector, flattened, precision=lax.Precision.HIGHEST)

        contrib = spread_updates(
            lax.all_gather(off_blocks[first_row:end_row], "rhs", axis=2, tiled=True), jnp.int32(0)
        )
        acc_local = acc_local.at[end_row:].add(contrib[: sub_count - end_row])
        acc_top = acc_top + contrib[sub_count - end_row :]
    inverse_rows = top_inv.reshape(1, 1, top_inv.shape[1], panel_width)
    top_full, inv_full = (
        lax.all_gather(top_factor, "rhs", axis=2, tiled=True),
        lax.all_gather(inverse_rows, "rhs", axis=2, tiled=True),
    )
    position = lax.axis_index("row")
    own_sum = lax.psum_scatter(
        acc_top.astype(jnp.bfloat16), "row", scatter_dimension=0, tiled=True
    ).astype(jnp.float32)
    base_value = top_rhs[0].astype(jnp.float32) - own_sum[0]

    def top_step(step_index, carry):
        carried, own_solution = carry
        residual_rows = (base_value - carried).astype(jnp.bfloat16)
        candidate = jnp.dot(
            inv_full[0, 0], residual_rows, preferred_element_type=jnp.float32
        ).astype(jnp.bfloat16)
        solution = spread(candidate, "row", step_index)
        own_solution = jnp.where(position == step_index, solution, own_solution)
        coupling_matrix = lax.dynamic_index_in_dim(top_full[0], step_index, 0, keepdims=False)
        update = jnp.dot(coupling_matrix, solution, preferred_element_type=jnp.float32)
        carried = carried + jnp.where(step_index < position, update, 0.0)
        return (carried, own_solution)

    initial_state = (
        jnp.zeros((panel_width, columns), jnp.float32),
        jnp.zeros((panel_width, columns), jnp.bfloat16),
    )
    own_separator = lax.fori_loop(0, top_count, top_step, initial_state)[1][None]
    return (jnp.concatenate(solved, axis=0), own_separator)


CHUNK = 3
LINE = 4
HOP = 1
READY = HOP * (LINE - 1) + 1
LEFT, RIGHT, ACROSS = 0, 1, 2
MESH = pl.DeviceIdType.MESH


def detour(k):
    return lax.rem(k, 6) == 3


def times_turned(left, right):
    return lax.dot_general(left, right, (((1,), (1,)), ((), ())), preferred_element_type=jnp.float32)


def relay_kernel(
    rows, rhs_hbm, top_rhs_hbm, diag_hbm, top_inv_hbm, off_hbm, top_factor_hbm, targets,
    out_hbm, top_out_hbm,
    held, held_top, rhs, top_rhs, sol, acc, prod, part, parts, top_sol,
    turned, top_rhs_turned, gathered, top_out,
    load_sem, out_sem, send_sem, recv_sem, row_send, row_recv, top_send, top_recv,
):
    sub, width, columns = rhs.shape
    chunks = 1 + sub // CHUNK
    cand = sub + rows
    share = columns // rows
    row, me = lax.axis_index("row"), lax.axis_index("rhs")
    z, y = me // 2, lax.rem(me, 2)
    targets_of = {LEFT: me - 2, RIGHT: me + 2, ACROSS: z * 2 + 1 - y}
    peers = [lax.rem(row + p, rows) for p in range(1, rows)]

    def load(index, src, dst):
        return pltpu.make_async_copy(src, dst, load_sem.at[index])

    early, late = pl.ds(0, CHUNK), pl.ds(CHUNK, sub - CHUNK)
    first_loads = [
        load(0, top_inv_hbm.at[0], held_top.at[row, me, 0]),
        load(1, top_factor_hbm.at[0], held_top.at[row, me, pl.ds(1, 4)]),
        load(2, diag_hbm.at[early], held.at[me, early, 0]),
        load(3, off_hbm.at[early], held.at[me, early, pl.ds(1, 4)]),
        load(4, top_rhs_hbm.at[0], top_rhs.at[row]),
    ]
    next_loads = [
        load(5, diag_hbm.at[late], held.at[me, late, 0]),
        load(6, off_hbm.at[late], held.at[me, late, pl.ds(1, 4)]),
    ]
    rhs_load = load(7, rhs_hbm, rhs)

    barrier = pltpu.get_barrier_semaphore()
    for peer in peers:
        pl.semaphore_signal(barrier, inc=1, device_id=(peer, me), device_id_type=MESH)
    pl.semaphore_signal(barrier, inc=1, device_id=(row, targets_of[ACROSS]), device_id_type=MESH)

    @pl.when(z > 0)
    def _():
        pl.semaphore_signal(barrier, inc=1, device_id=(row, targets_of[LEFT]), device_id_type=MESH)

    @pl.when(z < LINE - 1)
    def _():
        pl.semaphore_signal(barrier, inc=1, device_id=(row, targets_of[RIGHT]), device_id_type=MESH)

    for copy in first_loads + next_loads + [rhs_load]:
        copy.start()

    def clear(c, carry):
        acc[c] = jnp.zeros((width, columns), jnp.float32)
        return carry

    lax.fori_loop(0, cand, clear, 0)
    for u in range(CHUNK):
        prod[u * 5 + 4] = jnp.zeros((width, columns), jnp.float32)

    ends = jnp.where(z == 0, 1, 0) + jnp.where(z == LINE - 1, 1, 0)
    pl.semaphore_wait(barrier, rows + 2 - ends)
    for copy in first_loads:
        copy.wait()

    def row_copy(kind, p, src, dst):
        return pltpu.make_async_remote_copy(
            src_ref=src, dst_ref=dst, send_sem=row_send.at[kind, p], recv_sem=row_recv.at[kind, row],
            device_id=(peers[p], me), device_id_type=MESH,
        )

    def row_arrival(kind, p, dst):
        return pltpu.make_async_remote_copy(
            src_ref=dst, dst_ref=dst, send_sem=row_send.at[kind, p], recv_sem=row_recv.at[kind, peers[p]],
            device_id=(peers[p], me), device_id_type=MESH,
        )

    for p in range(rows - 1):
        row_copy(0, p, top_rhs.at[row], top_rhs.at[row]).start()

    def either(k, src, count, act):
        @pl.when(k == 0)
        def _():
            act(held_top.at[row, pl.ds(src, count)])

        @pl.when(k > 0)
        def _():
            act(held.at[pl.ds(src, count), pl.ds((k - 1) * CHUNK, CHUNK)])

    def describe(ref, k, src, way):
        return pltpu.make_async_remote_copy(
            src_ref=ref, dst_ref=ref, send_sem=send_sem.at[way, k], recv_sem=recv_sem.at[k, src],
            device_id=(row, targets_of[way]), device_id_type=MESH,
        )

    def relay(k, src, wait, ways):
        def act(ref):
            if wait:
                describe(ref, k, src, ACROSS).wait_recv()
            for way, wanted in ways:
                @pl.when(wanted)
                def _(way=way):
                    describe(ref, k, src, way).start()

        either(k, src, 1, act)

    def drain(k):
        around = detour(k)
        sends = {
            LEFT: jnp.where(z > 0, (LINE - z) * jnp.where(around, 2, 1), 0),
            RIGHT: jnp.where(z < LINE - 1, (z + 1) * jnp.where(around, 2, 1), 0),
            ACROSS: jnp.where(around, 1, LINE),
        }
        for way, sizes in ((LEFT, (1, 2, 3, 4, 6)), (RIGHT, (1, 2, 3, 4, 6)), (ACROSS, (1, LINE))):
            for size in sizes:
                @pl.when(sends[way] == size)
                def _(way=way, size=size):
                    either(k, 0, size, lambda ref: describe(ref, k, 0, way).wait_send())

    def solve(k):
        first = (k - 1) * CHUNK
        half = LEAF + LEAF // 2
        codes = [[targets[j, first + u] for j in range(4)] for u in range(CHUNK)]
        residuals = [
            (rhs[first + u].astype(jnp.float32) - acc[first + u]).astype(jnp.bfloat16) for u in range(CHUNK)
        ]
        solved = [
            jnp.dot(held[:, first + u, 0].reshape(width, width), residuals[u], preferred_element_type=jnp.float32)
            for u in range(CHUNK)
        ]
        solved = [x.astype(jnp.bfloat16) for x in solved]
        for u in range(CHUNK):
            sol[first + u] = solved[u]
        for u in range(CHUNK):
            blocks = [held[:, first + u, 1 + j].reshape(width, width) for j in range(4)]
            updates = jnp.dot(jnp.concatenate(blocks, axis=0), solved[u], preferred_element_type=jnp.float32)
            prod[pl.ds(u * 5, 4)] = updates.reshape(4, width, columns)
        pltpu.make_async_copy(sol.at[pl.ds(first, CHUNK)], out_hbm.at[pl.ds(first, CHUNK)], out_sem.at[0]).start()

        least = jnp.where(first < LEAF, LEAF, jnp.where(first < half, half, sub))

        def add(pair, carry):
            for c in (least + 2 * pair, least + 2 * pair + 1):
                total = acc[c]
                for u in range(CHUNK):
                    slot = jnp.int32(u * 5 + 4)
                    for j in range(4):
                        slot = jnp.where(codes[u][j] == c, u * 5 + j, slot)
                    total = total + prod[slot]
                acc[c] = total
            return carry

        lax.fori_loop(0, (cand - least) // 2, add, 0)

    def step(i, carry):
        for d in range(LINE):
            k = i - HOP * d

            @pl.when((k >= 0) & (k < chunks))
            def _(k=k, d=d):
                straight = jnp.logical_not(detour(k))
                if d == 0:
                    @pl.when(k == 2)
                    def _():
                        for copy in next_loads:
                            copy.wait()

                    relay(k, me, False, ((LEFT, z > 0), (RIGHT, z < LINE - 1), (ACROSS, z >= 0)))
                else:
                    @pl.when(z >= d)
                    def _():
                        relay(k, me - 2 * d, True, ((RIGHT, z < LINE - 1), (ACROSS, straight)))

                    @pl.when(z + d < LINE)
                    def _():
                        relay(k, me + 2 * d, True, ((LEFT, z > 0), (ACROSS, straight)))

            k = i - HOP * d - 1

            @pl.when((k >= 0) & (k < chunks) & detour(k))
            def _(k=k, d=d):
                far = targets_of[ACROSS]
                if d == 0:
                    relay(k, far, True, ((LEFT, z > 0), (RIGHT, z < LINE - 1)))
                else:
                    @pl.when(z >= d)
                    def _():
                        relay(k, far - 2 * d, True, ((RIGHT, z < LINE - 1),))

                    @pl.when(z + d < LINE)
                    def _():
                        relay(k, far + 2 * d, True, ((LEFT, z > 0),))

        k = i - READY

        @pl.when(k >= 0)
        def _():
            @pl.when(jnp.logical_not(detour(k)))
            def _():
                for other in range(LINE):
                    relay(k, other * 2 + 1 - y, True, ())

            @pl.when(k == 0)
            def _():
                rhs_load.wait()
                for p in range(rows - 1):
                    row_arrival(0, p, top_rhs.at[peers[p]]).wait_recv()
                for t in range(rows):
                    top_rhs_turned[t] = top_rhs[t].astype(jnp.float32).T
                for p in range(rows - 1):
                    row_copy(1, p, held_top.at[row], held_top.at[row]).start()

            @pl.when(k > 0)
            def _():
                solve(k)

        @pl.when(i > READY)
        def _():
            drain(i - READY - 1)

        return carry

    steps = chunks + READY
    lax.fori_loop(0, steps, step, 0)

    mine = pl.ds(pl.multiple_of(row * share, share), share)
    for t in range(rows):
        turned[t] = acc[sub + t].T
        part[t] = turned[t].astype(jnp.bfloat16)
    slices = [part.at[:, pl.ds(pl.multiple_of(peer * share, share), share)] for peer in peers]
    for p in range(rows - 1):
        row_copy(2, p, slices[p], parts.at[row]).start()

    for p in range(rows - 1):
        row_arrival(1, p, held_top.at[peers[p]]).wait_recv()
    for p in range(rows - 1):
        row_arrival(2, p, parts.at[peers[p]]).wait_recv()

    def solved_copy(t):
        return pltpu.make_async_remote_copy(
            src_ref=top_sol.at[t], dst_ref=gathered.at[row], send_sem=top_send.at[t], recv_sem=top_recv.at[row],
            device_id=(t, me), device_id_type=MESH,
        )

    for t in range(rows):
        base = turned[t, mine]
        for p in range(rows - 1):
            base = base + parts[peers[p], t].astype(jnp.float32)
        base = top_rhs_turned[t, mine] - base
        for earlier in range(t):
            factor = held_top[t, :, 1 + earlier].reshape(width, width)
            base = base - times_turned(top_sol[earlier], factor)
        inverse = held_top[t, :, 0].reshape(width, width)
        top_sol[t] = times_turned(base.astype(jnp.bfloat16), inverse).astype(jnp.bfloat16)

        @pl.when(row != t)
        def _(t=t):
            solved_copy(t).start()

        @pl.when(row == t)
        def _(t=t):
            gathered[row] = top_sol[t]

    for p in range(rows - 1):
        pltpu.make_async_remote_copy(
            src_ref=top_sol.at[0], dst_ref=gathered.at[peers[p]], send_sem=top_send.at[0], recv_sem=top_recv.at[peers[p]],
            device_id=(peers[p], me), device_id_type=MESH,
        ).wait_recv()
    owned = gathered[...].reshape(columns, width).astype(jnp.float32)
    top_out[...] = owned.T.astype(jnp.bfloat16)
    last = pltpu.make_async_copy(top_out, top_out_hbm.at[0], out_sem.at[1])
    last.start()
    def drain_rest(k, carry):
        drain(k)
        return carry

    lax.fori_loop(chunks - 1, chunks, drain_rest, 0)
    for p in range(rows - 1):
        row_copy(0, p, top_rhs.at[row], top_rhs.at[row]).wait_send()
        row_copy(1, p, held_top.at[row], held_top.at[row]).wait_send()
        row_copy(2, p, slices[p], parts.at[row]).wait_send()
    for t in range(rows):
        @pl.when(row != t)
        def _(t=t):
            solved_copy(t).wait_send()
    pltpu.make_async_copy(sol, out_hbm, out_sem.at[0]).wait()
    last.wait()


def place_kernel(local_in, top_in, local_out, top_out, local_held, top_held, in_sem, out_sem):
    pieces = len(range(0, local_in.shape[0], 2 * CHUNK))
    size = local_in.shape[0] // pieces
    parts = [pl.ds(index * size, size) for index in range(pieces)]
    stages = [(local_in.at[part], local_held.at[part], local_out.at[part]) for part in parts]
    stages.append((top_in, top_held, top_out))
    fetches = [pltpu.make_async_copy(a, b, in_sem.at[index]) for index, (a, b, c) in enumerate(stages)]
    stores = [pltpu.make_async_copy(b, c, out_sem.at[index]) for index, (a, b, c) in enumerate(stages)]
    for fetch in fetches:
        fetch.start()
    for fetch, store in zip(fetches, stores):
        fetch.wait()
        store.start()
    for store in stores:
        store.wait()


def placed(local_solution, top_solution):
    pieces = len(range(0, local_solution.shape[0], 2 * CHUNK))
    return pl.pallas_call(
        place_kernel,
        out_shape=tuple(jax.ShapeDtypeStruct(x.shape, x.dtype) for x in (local_solution, top_solution)),
        in_specs=[pl.BlockSpec(memory_space=pl.ANY)] * 2,
        out_specs=(pl.BlockSpec(memory_space=pl.ANY),) * 2,
        scratch_shapes=[
            pltpu.VMEM(local_solution.shape, local_solution.dtype),
            pltpu.VMEM(top_solution.shape, top_solution.dtype),
            pltpu.SemaphoreType.DMA((1 + pieces,)),
            pltpu.SemaphoreType.DMA((1 + pieces,)),
        ],
        compiler_params=pltpu.CompilerParams(vmem_limit_bytes=60 * 1024 * 1024),
    )(local_solution, top_solution)


def relayed(local_rhs, top_rhs, diag_inv, top_inv, off_blocks, top_factor, targets):
    rows, ranks = lax.axis_size("row"), lax.axis_size("rhs")
    sub, width, columns = local_rhs.shape
    share = diag_inv.shape[1]
    chunks = 1 + sub // CHUNK
    bf16, f32 = jnp.bfloat16, jnp.float32
    solutions = pl.pallas_call(
        functools.partial(relay_kernel, rows),
        out_shape=(
            jax.ShapeDtypeStruct(local_rhs.shape, bf16),
            jax.ShapeDtypeStruct(top_rhs.shape, bf16),
        ),
        in_specs=[pl.BlockSpec(memory_space=pltpu.HBM)] * 6 + [pl.BlockSpec(memory_space=pltpu.SMEM)],
        out_specs=(pl.BlockSpec(memory_space=pl.ANY),) * 2,
        scratch_shapes=[
            pltpu.VMEM((ranks, sub, 5, share, width), bf16),
            pltpu.VMEM((rows, ranks, 5, share, width), bf16),
            pltpu.VMEM((sub, width, columns), bf16),
            pltpu.VMEM((rows, width, columns), bf16),
            pltpu.VMEM((sub, width, columns), bf16),
            pltpu.VMEM((sub + rows, width, columns), f32),
            pltpu.VMEM((5 * CHUNK, width, columns), f32),
            pltpu.VMEM((rows, width, columns), bf16),
            pltpu.VMEM((rows, rows, columns // rows, width), bf16),
            pltpu.VMEM((rows, columns // rows, width), bf16),
            pltpu.VMEM((rows, columns, width), f32),
            pltpu.VMEM((rows, columns, width), f32),
            pltpu.VMEM((rows, columns // rows, width), bf16),
            pltpu.VMEM((width, columns), bf16),
            pltpu.SemaphoreType.DMA((8,)),
            pltpu.SemaphoreType.DMA((2,)),
            pltpu.SemaphoreType.DMA((3, chunks)),
            pltpu.SemaphoreType.DMA((chunks, ranks)),
            pltpu.SemaphoreType.DMA((3, rows - 1)),
            pltpu.SemaphoreType.DMA((3, rows)),
            pltpu.SemaphoreType.DMA((rows,)),
            pltpu.SemaphoreType.DMA((rows,)),
        ],
        compiler_params=pltpu.CompilerParams(
            collective_id=0, has_side_effects=True, vmem_limit_bytes=60 * 1024 * 1024
        ),
        cost_estimate=pl.CostEstimate(
            flops=10 * sub * width * width * columns, bytes_accessed=4 * local_rhs.size + 2 * off_blocks.size, transcendentals=0
        ),
    )(local_rhs, top_rhs, diag_inv, top_inv, off_blocks, top_factor, targets.T)
    return placed(*solutions)


def solution(mesh):
    in_specs = (
        P("row", None, "rhs"),
        P("row", None, "rhs"),
        P("row", "rhs", None),
        P("row", "rhs", None),
        P("row", None, "rhs", None),
        P("row", None, "rhs", None),
        P("row", None),
    )
    out_specs = (P("row", None, "rhs"), P("row", None, "rhs"))
    body = relayed if mesh.shape["rhs"] == 2 * LINE else local
    return jax.shard_map(body, mesh=mesh, in_specs=in_specs, out_specs=out_specs, check_vma=False)
```

```python
import functools
import jax
import jax.numpy as jnp
from jax import lax
from jax.experimental import pallas as pl
from jax.experimental.pallas import tpu as pltpu
from jax.sharding import PartitionSpec as P

LEAF = 24


def spread(shard, axis, root):
    mine = lax.axis_index(axis) == root
    return lax.psum(jnp.where(mine, shard, jnp.zeros_like(shard)), axis)


def local(local_rhs, top_rhs, diag_inv, top_inv, off_blocks, top_factor, targets):
    sub_count = local_rhs.shape[0]
    panel_width = local_rhs.shape[1]
    columns = local_rhs.shape[2]
    top_count = lax.axis_size("row")
    cand_count = sub_count + top_count
    acc_local = jnp.zeros((sub_count, panel_width, columns), jnp.float32)
    acc_top = jnp.zeros((top_count, panel_width, columns), jnp.float32)
    level_ranges = ((0, LEAF), (LEAF, LEAF + LEAF // 2), (LEAF + LEAF // 2, sub_count))
    solved = []
    for first_row, end_row in level_ranges:
        residual_rows = (
            local_rhs[first_row:end_row].astype(jnp.float32) - acc_local[first_row:end_row]
        ).astype(jnp.bfloat16)

        def apply_inverse(slice_part, offset, residual_rows=residual_rows):
            return jnp.einsum(
                "jxm,jme->jxe", slice_part, residual_rows, preferred_element_type=jnp.float32
            )

        level_partial = apply_inverse(
            lax.all_gather(diag_inv[first_row:end_row], "rhs", axis=1, tiled=True), jnp.int32(0)
        ).astype(jnp.bfloat16)
        solved.append(level_partial)
        target_codes = targets[first_row:end_row].reshape(-1)
        later_count = cand_count - end_row
        selector = (
            jnp.arange(later_count, dtype=jnp.int32)[:, None] == target_codes[None, :] - end_row
        ).astype(jnp.float32)

        def spread_updates(slice_part, offset, level_partial=level_partial, selector=selector):
            products = jnp.einsum(
                "yiko,yoq->yikq", slice_part, level_partial, preferred_element_type=jnp.float32
            )
            flattened = products.reshape(selector.shape[1], slice_part.shape[2], columns)
            return jnp.einsum("cn,nar->car", selector, flattened, precision=lax.Precision.HIGHEST)

        contrib = spread_updates(
            lax.all_gather(off_blocks[first_row:end_row], "rhs", axis=2, tiled=True), jnp.int32(0)
        )
        acc_local = acc_local.at[end_row:].add(contrib[: sub_count - end_row])
        acc_top = acc_top + contrib[sub_count - end_row :]
    inverse_rows = top_inv.reshape(1, 1, top_inv.shape[1], panel_width)
    top_full, inv_full = (
        lax.all_gather(top_factor, "rhs", axis=2, tiled=True),
        lax.all_gather(inverse_rows, "rhs", axis=2, tiled=True),
    )
    position = lax.axis_index("row")
    own_sum = lax.psum_scatter(
        acc_top.astype(jnp.bfloat16), "row", scatter_dimension=0, tiled=True
    ).astype(jnp.float32)
    base_value = top_rhs[0].astype(jnp.float32) - own_sum[0]

    def top_step(step_index, carry):
        carried, own_solution = carry
        residual_rows = (base_value - carried).astype(jnp.bfloat16)
        candidate = jnp.dot(
            inv_full[0, 0], residual_rows, preferred_element_type=jnp.float32
        ).astype(jnp.bfloat16)
        solution = spread(candidate, "row", step_index)
        own_solution = jnp.where(position == step_index, solution, own_solution)
        coupling_matrix = lax.dynamic_index_in_dim(top_full[0], step_index, 0, keepdims=False)
        update = jnp.dot(coupling_matrix, solution, preferred_element_type=jnp.float32)
        carried = carried + jnp.where(step_index < position, update, 0.0)
        return (carried, own_solution)

    initial_state = (
        jnp.zeros((panel_width, columns), jnp.float32),
        jnp.zeros((panel_width, columns), jnp.bfloat16),
    )
    own_separator = lax.fori_loop(0, top_count, top_step, initial_state)[1][None]
    return (jnp.concatenate(solved, axis=0), own_separator)


CHUNK = 3
LINE = 4
HOP = 1
READY = HOP * (LINE - 1) + 1
LEFT, RIGHT, ACROSS = 0, 1, 2
MESH = pl.DeviceIdType.MESH


def detour(k):
    return (k > 0) & (lax.rem(k, 2) == 0)


def times_turned(left, right):
    return lax.dot_general(left, right, (((1,), (1,)), ((), ())), preferred_element_type=jnp.float32)


def relay_kernel(
    rows, rhs_hbm, top_rhs_hbm, diag_hbm, top_inv_hbm, off_hbm, top_factor_hbm, targets,
    out_hbm, top_out_hbm,
    held, held_top, rhs, top_rhs, sol, acc, prod, part, parts, top_sol,
    turned, top_rhs_turned, gathered, top_out,
    load_sem, out_sem, send_sem, recv_sem, row_send, row_recv, top_send, top_recv,
):
    sub, width, columns = rhs.shape
    chunks = 1 + sub // CHUNK
    cand = sub + rows
    share = columns // rows
    row, me = lax.axis_index("row"), lax.axis_index("rhs")
    z, y = me // 2, lax.rem(me, 2)
    targets_of = {LEFT: me - 2, RIGHT: me + 2, ACROSS: z * 2 + 1 - y}
    peers = [lax.rem(row + p, rows) for p in range(1, rows)]

    def load(index, src, dst):
        return pltpu.make_async_copy(src, dst, load_sem.at[index])

    early, late = pl.ds(0, CHUNK), pl.ds(CHUNK, sub - CHUNK)
    first_loads = [
        load(0, top_inv_hbm.at[0], held_top.at[row, me, 0]),
        load(1, top_factor_hbm.at[0], held_top.at[row, me, pl.ds(1, 4)]),
        load(2, diag_hbm.at[early], held.at[me, early, 0]),
        load(3, off_hbm.at[early], held.at[me, early, pl.ds(1, 4)]),
        load(4, top_rhs_hbm.at[0], top_rhs.at[row]),
    ]
    next_loads = [
        load(5, diag_hbm.at[late], held.at[me, late, 0]),
        load(6, off_hbm.at[late], held.at[me, late, pl.ds(1, 4)]),
    ]
    rhs_load = load(7, rhs_hbm, rhs)

    barrier = pltpu.get_barrier_semaphore()
    for peer in peers:
        pl.semaphore_signal(barrier, inc=1, device_id=(peer, me), device_id_type=MESH)
    pl.semaphore_signal(barrier, inc=1, device_id=(row, targets_of[ACROSS]), device_id_type=MESH)

    @pl.when(z > 0)
    def _():
        pl.semaphore_signal(barrier, inc=1, device_id=(row, targets_of[LEFT]), device_id_type=MESH)

    @pl.when(z < LINE - 1)
    def _():
        pl.semaphore_signal(barrier, inc=1, device_id=(row, targets_of[RIGHT]), device_id_type=MESH)

    for copy in first_loads + next_loads + [rhs_load]:
        copy.start()

    def clear(c, carry):
        acc[c] = jnp.zeros((width, columns), jnp.float32)
        return carry

    lax.fori_loop(0, cand, clear, 0)
    for u in range(CHUNK):
        prod[u * 5 + 4] = jnp.zeros((width, columns), jnp.float32)

    ends = jnp.where(z == 0, 1, 0) + jnp.where(z == LINE - 1, 1, 0)
    pl.semaphore_wait(barrier, rows + 2 - ends)
    for copy in first_loads:
        copy.wait()

    def row_copy(kind, p, src, dst):
        return pltpu.make_async_remote_copy(
            src_ref=src, dst_ref=dst, send_sem=row_send.at[kind, p], recv_sem=row_recv.at[kind, row],
            device_id=(peers[p], me), device_id_type=MESH,
        )

    def row_arrival(kind, p, dst):
        return pltpu.make_async_remote_copy(
            src_ref=dst, dst_ref=dst, send_sem=row_send.at[kind, p], recv_sem=row_recv.at[kind, peers[p]],
            device_id=(peers[p], me), device_id_type=MESH,
        )

    for p in range(rows - 1):
        row_copy(0, p, top_rhs.at[row], top_rhs.at[row]).start()

    def straight_piece(k, src, count, act):
        first = (k - 1) * CHUNK

        @pl.when(k == 0)
        def _():
            act(held_top.at[row, pl.ds(src, count)])

        @pl.when((k > 0) & jnp.logical_not(detour(k)))
        def _():
            act(held.at[pl.ds(src, count), pl.ds(first, CHUNK)])

        @pl.when(detour(k))
        def _():
            act(held.at[pl.ds(src, count), pl.ds(first, CHUNK - 1)])

    def around_piece(k, src, count, act):
        @pl.when(detour(k))
        def _():
            act(held.at[pl.ds(src, count), pl.ds(k * CHUNK - 1, 1)])

    pieces = (straight_piece, around_piece)

    def describe(ref, kind, k, src, way):
        return pltpu.make_async_remote_copy(
            src_ref=ref, dst_ref=ref, send_sem=send_sem.at[kind, way, k], recv_sem=recv_sem.at[kind, k, src],
            device_id=(row, targets_of[way]), device_id_type=MESH,
        )

    def relay(kind, k, src, wait, ways):
        def act(ref):
            if wait:
                describe(ref, kind, k, src, ACROSS).wait_recv()
            for way, wanted in ways:
                @pl.when(wanted)
                def _(way=way):
                    describe(ref, kind, k, src, way).start()

        pieces[kind](k, src, 1, act)

    def drain(k):
        left = jnp.where(z > 0, LINE - z, 0)
        right = jnp.where(z < LINE - 1, z + 1, 0)
        for kind in range(2):
            for way, sends in ((LEFT, left), (RIGHT, right), (ACROSS, LINE)):
                for count in (LINE,) if way == ACROSS else (1, 2, 3):
                    size = (1 if way == ACROSS else 2 * count) if kind else count

                    @pl.when(sends == count)
                    def _(kind=kind, way=way, size=size):
                        pieces[kind](k, 0, size, lambda ref: describe(ref, kind, k, 0, way).wait_send())

    def solve(k):
        first = (k - 1) * CHUNK
        half = LEAF + LEAF // 2
        codes = [[targets[j, first + u] for j in range(4)] for u in range(CHUNK)]
        residuals = [
            (rhs[first + u].astype(jnp.float32) - acc[first + u]).astype(jnp.bfloat16) for u in range(CHUNK)
        ]
        solved = [
            jnp.dot(held[:, first + u, 0].reshape(width, width), residuals[u], preferred_element_type=jnp.float32)
            for u in range(CHUNK)
        ]
        solved = [x.astype(jnp.bfloat16) for x in solved]
        for u in range(CHUNK):
            sol[first + u] = solved[u]
        for u in range(CHUNK):
            blocks = [held[:, first + u, 1 + j].reshape(width, width) for j in range(4)]
            updates = jnp.dot(jnp.concatenate(blocks, axis=0), solved[u], preferred_element_type=jnp.float32)
            prod[pl.ds(u * 5, 4)] = updates.reshape(4, width, columns)
        pltpu.make_async_copy(sol.at[pl.ds(first, CHUNK)], out_hbm.at[pl.ds(first, CHUNK)], out_sem.at[0]).start()

        least = jnp.where(first < LEAF, LEAF, jnp.where(first < half, half, sub))

        def add(pair, carry):
            for c in (least + 2 * pair, least + 2 * pair + 1):
                total = acc[c]
                for u in range(CHUNK):
                    slot = jnp.int32(u * 5 + 4)
                    for j in range(4):
                        slot = jnp.where(codes[u][j] == c, u * 5 + j, slot)
                    total = total + prod[slot]
                acc[c] = total
            return carry

        lax.fori_loop(0, (cand - least) // 2, add, 0)

    def step(i, carry):
        for d in range(LINE):
            k = i - HOP * d

            @pl.when((k >= 0) & (k < chunks))
            def _(k=k, d=d):
                if d == 0:
                    @pl.when(k == 2)
                    def _():
                        for copy in next_loads:
                            copy.wait()

                    for kind in range(2):
                        relay(kind, k, me, False, ((LEFT, z > 0), (RIGHT, z < LINE - 1), (ACROSS, z >= 0)))
                else:
                    @pl.when(z >= d)
                    def _():
                        relay(0, k, me - 2 * d, True, ((RIGHT, z < LINE - 1), (ACROSS, z >= 0)))
                        relay(1, k, me - 2 * d, True, ((RIGHT, z < LINE - 1),))

                    @pl.when(z + d < LINE)
                    def _():
                        relay(0, k, me + 2 * d, True, ((LEFT, z > 0), (ACROSS, z >= 0)))
                        relay(1, k, me + 2 * d, True, ((LEFT, z > 0),))

            k = i - HOP * d - 1

            @pl.when((k >= 0) & (k < chunks))
            def _(k=k, d=d):
                far = targets_of[ACROSS]
                if d == 0:
                    relay(1, k, far, True, ((LEFT, z > 0), (RIGHT, z < LINE - 1)))
                else:
                    @pl.when(z >= d)
                    def _():
                        relay(1, k, far - 2 * d, True, ((RIGHT, z < LINE - 1),))

                    @pl.when(z + d < LINE)
                    def _():
                        relay(1, k, far + 2 * d, True, ((LEFT, z > 0),))

        k = i - READY

        @pl.when(k >= 0)
        def _():
            for other in range(LINE):
                relay(0, k, other * 2 + 1 - y, True, ())

            @pl.when(k == 0)
            def _():
                rhs_load.wait()
                for p in range(rows - 1):
                    row_arrival(0, p, top_rhs.at[peers[p]]).wait_recv()
                for t in range(rows):
                    top_rhs_turned[t] = top_rhs[t].astype(jnp.float32).T
                for p in range(rows - 1):
                    row_copy(1, p, held_top.at[row], held_top.at[row]).start()

            @pl.when(k > 0)
            def _():
                solve(k)

        @pl.when(i > READY)
        def _():
            drain(i - READY - 1)

        return carry

    steps = chunks + READY
    lax.fori_loop(0, steps, step, 0)

    mine = pl.ds(pl.multiple_of(row * share, share), share)
    for t in range(rows):
        turned[t] = acc[sub + t].T
        part[t] = turned[t].astype(jnp.bfloat16)
    slices = [part.at[:, pl.ds(pl.multiple_of(peer * share, share), share)] for peer in peers]
    for p in range(rows - 1):
        row_copy(2, p, slices[p], parts.at[row]).start()

    for p in range(rows - 1):
        row_arrival(1, p, held_top.at[peers[p]]).wait_recv()
    for p in range(rows - 1):
        row_arrival(2, p, parts.at[peers[p]]).wait_recv()

    def solved_copy(t):
        return pltpu.make_async_remote_copy(
            src_ref=top_sol.at[t], dst_ref=gathered.at[row], send_sem=top_send.at[t], recv_sem=top_recv.at[row],
            device_id=(t, me), device_id_type=MESH,
        )

    for t in range(rows):
        base = turned[t, mine]
        for p in range(rows - 1):
            base = base + parts[peers[p], t].astype(jnp.float32)
        base = top_rhs_turned[t, mine] - base
        for earlier in range(t):
            factor = held_top[t, :, 1 + earlier].reshape(width, width)
            base = base - times_turned(top_sol[earlier], factor)
        inverse = held_top[t, :, 0].reshape(width, width)
        top_sol[t] = times_turned(base.astype(jnp.bfloat16), inverse).astype(jnp.bfloat16)

        @pl.when(row != t)
        def _(t=t):
            solved_copy(t).start()

        @pl.when(row == t)
        def _(t=t):
            gathered[row] = top_sol[t]

    for p in range(rows - 1):
        pltpu.make_async_remote_copy(
            src_ref=top_sol.at[0], dst_ref=gathered.at[peers[p]], send_sem=top_send.at[0], recv_sem=top_recv.at[peers[p]],
            device_id=(peers[p], me), device_id_type=MESH,
        ).wait_recv()
    owned = gathered[...].reshape(columns, width).astype(jnp.float32)
    top_out[...] = owned.T.astype(jnp.bfloat16)
    last = pltpu.make_async_copy(top_out, top_out_hbm.at[0], out_sem.at[1])
    last.start()
    def drain_rest(k, carry):
        drain(k)
        return carry

    lax.fori_loop(chunks - 1, chunks, drain_rest, 0)
    for p in range(rows - 1):
        row_copy(0, p, top_rhs.at[row], top_rhs.at[row]).wait_send()
        row_copy(1, p, held_top.at[row], held_top.at[row]).wait_send()
        row_copy(2, p, slices[p], parts.at[row]).wait_send()
    for t in range(rows):
        @pl.when(row != t)
        def _(t=t):
            solved_copy(t).wait_send()
    pltpu.make_async_copy(sol, out_hbm, out_sem.at[0]).wait()
    last.wait()


def place_kernel(local_in, top_in, local_out, top_out, local_held, top_held, in_sem, out_sem):
    pieces = len(range(0, local_in.shape[0], 2 * CHUNK))
    size = local_in.shape[0] // pieces
    parts = [pl.ds(index * size, size) for index in range(pieces)]
    stages = [(local_in.at[part], local_held.at[part], local_out.at[part]) for part in parts]
    stages.append((top_in, top_held, top_out))
    fetches = [pltpu.make_async_copy(a, b, in_sem.at[index]) for index, (a, b, c) in enumerate(stages)]
    stores = [pltpu.make_async_copy(b, c, out_sem.at[index]) for index, (a, b, c) in enumerate(stages)]
    for fetch in fetches:
        fetch.start()
    for fetch, store in zip(fetches, stores):
        fetch.wait()
        store.start()
    for store in stores:
        store.wait()


def placed(local_solution, top_solution):
    pieces = len(range(0, local_solution.shape[0], 2 * CHUNK))
    return pl.pallas_call(
        place_kernel,
        out_shape=tuple(jax.ShapeDtypeStruct(x.shape, x.dtype) for x in (local_solution, top_solution)),
        in_specs=[pl.BlockSpec(memory_space=pl.ANY)] * 2,
        out_specs=(pl.BlockSpec(memory_space=pl.ANY),) * 2,
        scratch_shapes=[
            pltpu.VMEM(local_solution.shape, local_solution.dtype),
            pltpu.VMEM(top_solution.shape, top_solution.dtype),
            pltpu.SemaphoreType.DMA((1 + pieces,)),
            pltpu.SemaphoreType.DMA((1 + pieces,)),
        ],
        compiler_params=pltpu.CompilerParams(vmem_limit_bytes=60 * 1024 * 1024),
    )(local_solution, top_solution)


def relayed(local_rhs, top_rhs, diag_inv, top_inv, off_blocks, top_factor, targets):
    rows, ranks = lax.axis_size("row"), lax.axis_size("rhs")
    sub, width, columns = local_rhs.shape
    share = diag_inv.shape[1]
    chunks = 1 + sub // CHUNK
    bf16, f32 = jnp.bfloat16, jnp.float32
    solutions = pl.pallas_call(
        functools.partial(relay_kernel, rows),
        out_shape=(
            jax.ShapeDtypeStruct(local_rhs.shape, bf16),
            jax.ShapeDtypeStruct(top_rhs.shape, bf16),
        ),
        in_specs=[pl.BlockSpec(memory_space=pltpu.HBM)] * 6 + [pl.BlockSpec(memory_space=pltpu.SMEM)],
        out_specs=(pl.BlockSpec(memory_space=pl.ANY),) * 2,
        scratch_shapes=[
            pltpu.VMEM((ranks, sub, 5, share, width), bf16),
            pltpu.VMEM((rows, ranks, 5, share, width), bf16),
            pltpu.VMEM((sub, width, columns), bf16),
            pltpu.VMEM((rows, width, columns), bf16),
            pltpu.VMEM((sub, width, columns), bf16),
            pltpu.VMEM((sub + rows, width, columns), f32),
            pltpu.VMEM((5 * CHUNK, width, columns), f32),
            pltpu.VMEM((rows, width, columns), bf16),
            pltpu.VMEM((rows, rows, columns // rows, width), bf16),
            pltpu.VMEM((rows, columns // rows, width), bf16),
            pltpu.VMEM((rows, columns, width), f32),
            pltpu.VMEM((rows, columns, width), f32),
            pltpu.VMEM((rows, columns // rows, width), bf16),
            pltpu.VMEM((width, columns), bf16),
            pltpu.SemaphoreType.DMA((8,)),
            pltpu.SemaphoreType.DMA((2,)),
            pltpu.SemaphoreType.DMA((2, 3, chunks)),
            pltpu.SemaphoreType.DMA((2, chunks, ranks)),
            pltpu.SemaphoreType.DMA((3, rows - 1)),
            pltpu.SemaphoreType.DMA((3, rows)),
            pltpu.SemaphoreType.DMA((rows,)),
            pltpu.SemaphoreType.DMA((rows,)),
        ],
        compiler_params=pltpu.CompilerParams(
            collective_id=0, has_side_effects=True, vmem_limit_bytes=60 * 1024 * 1024
        ),
        cost_estimate=pl.CostEstimate(
            flops=10 * sub * width * width * columns, bytes_accessed=4 * local_rhs.size + 2 * off_blocks.size, transcendentals=0
        ),
    )(local_rhs, top_rhs, diag_inv, top_inv, off_blocks, top_factor, targets.T)
    return placed(*solutions)


def solution(mesh):
    in_specs = (
        P("row", None, "rhs"),
        P("row", None, "rhs"),
        P("row", "rhs", None),
        P("row", "rhs", None),
        P("row", None, "rhs", None),
        P("row", None, "rhs", None),
        P("row", None),
    )
    out_specs = (P("row", None, "rhs"), P("row", None, "rhs"))
    body = relayed if mesh.shape["rhs"] == 2 * LINE else local
    return jax.shard_map(body, mesh=mesh, in_specs=in_specs, out_specs=out_specs, check_vma=False)
```

```python
import functools
import jax
import jax.numpy as jnp
from jax import lax
from jax.experimental import pallas as pl
from jax.experimental.pallas import tpu as pltpu
from jax.sharding import PartitionSpec as P

LEAF = 24


def spread(shard, axis, root):
    mine = lax.axis_index(axis) == root
    return lax.psum(jnp.where(mine, shard, jnp.zeros_like(shard)), axis)


def local(local_rhs, top_rhs, diag_inv, top_inv, off_blocks, top_factor, targets):
    sub_count = local_rhs.shape[0]
    panel_width = local_rhs.shape[1]
    columns = local_rhs.shape[2]
    top_count = lax.axis_size("row")
    cand_count = sub_count + top_count
    acc_local = jnp.zeros((sub_count, panel_width, columns), jnp.float32)
    acc_top = jnp.zeros((top_count, panel_width, columns), jnp.float32)
    level_ranges = ((0, LEAF), (LEAF, LEAF + LEAF // 2), (LEAF + LEAF // 2, sub_count))
    solved = []
    for first_row, end_row in level_ranges:
        residual_rows = (
            local_rhs[first_row:end_row].astype(jnp.float32) - acc_local[first_row:end_row]
        ).astype(jnp.bfloat16)

        def apply_inverse(slice_part, offset, residual_rows=residual_rows):
            return jnp.einsum(
                "jxm,jme->jxe", slice_part, residual_rows, preferred_element_type=jnp.float32
            )

        level_partial = apply_inverse(
            lax.all_gather(diag_inv[first_row:end_row], "rhs", axis=1, tiled=True), jnp.int32(0)
        ).astype(jnp.bfloat16)
        solved.append(level_partial)
        target_codes = targets[first_row:end_row].reshape(-1)
        later_count = cand_count - end_row
        selector = (
            jnp.arange(later_count, dtype=jnp.int32)[:, None] == target_codes[None, :] - end_row
        ).astype(jnp.float32)

        def spread_updates(slice_part, offset, level_partial=level_partial, selector=selector):
            products = jnp.einsum(
                "yiko,yoq->yikq", slice_part, level_partial, preferred_element_type=jnp.float32
            )
            flattened = products.reshape(selector.shape[1], slice_part.shape[2], columns)
            return jnp.einsum("cn,nar->car", selector, flattened, precision=lax.Precision.HIGHEST)

        contrib = spread_updates(
            lax.all_gather(off_blocks[first_row:end_row], "rhs", axis=2, tiled=True), jnp.int32(0)
        )
        acc_local = acc_local.at[end_row:].add(contrib[: sub_count - end_row])
        acc_top = acc_top + contrib[sub_count - end_row :]
    inverse_rows = top_inv.reshape(1, 1, top_inv.shape[1], panel_width)
    top_full, inv_full = (
        lax.all_gather(top_factor, "rhs", axis=2, tiled=True),
        lax.all_gather(inverse_rows, "rhs", axis=2, tiled=True),
    )
    position = lax.axis_index("row")
    own_sum = lax.psum_scatter(
        acc_top.astype(jnp.bfloat16), "row", scatter_dimension=0, tiled=True
    ).astype(jnp.float32)
    base_value = top_rhs[0].astype(jnp.float32) - own_sum[0]

    def top_step(step_index, carry):
        carried, own_solution = carry
        residual_rows = (base_value - carried).astype(jnp.bfloat16)
        candidate = jnp.dot(
            inv_full[0, 0], residual_rows, preferred_element_type=jnp.float32
        ).astype(jnp.bfloat16)
        solution = spread(candidate, "row", step_index)
        own_solution = jnp.where(position == step_index, solution, own_solution)
        coupling_matrix = lax.dynamic_index_in_dim(top_full[0], step_index, 0, keepdims=False)
        update = jnp.dot(coupling_matrix, solution, preferred_element_type=jnp.float32)
        carried = carried + jnp.where(step_index < position, update, 0.0)
        return (carried, own_solution)

    initial_state = (
        jnp.zeros((panel_width, columns), jnp.float32),
        jnp.zeros((panel_width, columns), jnp.bfloat16),
    )
    own_separator = lax.fori_loop(0, top_count, top_step, initial_state)[1][None]
    return (jnp.concatenate(solved, axis=0), own_separator)


CHUNK = 3
LINE = 4
HOP = 1
READY = HOP * (LINE - 1) + 1
LEFT, RIGHT, ACROSS = 0, 1, 2
MESH = pl.DeviceIdType.MESH


def detour(k):
    return lax.rem(k, 6) == 3


def relay_kernel(
    rows, rhs_hbm, top_rhs_hbm, diag_hbm, top_inv_hbm, off_hbm, top_factor_hbm, targets,
    out_hbm, top_out_hbm,
    held, held_top, rhs, top_rhs, sol, acc, prod, part, parts, top_sol,
    turned, top_rhs_turned, gathered, top_out, top_turned,
    load_sem, out_sem, send_sem, recv_sem, row_send, row_recv, top_send, top_recv,
):
    sub, width, columns = rhs.shape
    chunks = 1 + sub // CHUNK
    cand = sub + rows
    share = columns // rows
    row, me = lax.axis_index("row"), lax.axis_index("rhs")
    z, y = me // 2, lax.rem(me, 2)
    targets_of = {LEFT: me - 2, RIGHT: me + 2, ACROSS: z * 2 + 1 - y}
    peers = [lax.rem(row + p, rows) for p in range(1, rows)]

    def load(index, src, dst):
        return pltpu.make_async_copy(src, dst, load_sem.at[index])

    early, late = pl.ds(0, CHUNK), pl.ds(CHUNK, sub - CHUNK)
    first_loads = [
        load(0, top_inv_hbm.at[0], held_top.at[row, me, 0]),
        load(1, top_factor_hbm.at[0], held_top.at[row, me, pl.ds(1, 4)]),
        load(2, diag_hbm.at[early], held.at[me, early, 0]),
        load(3, off_hbm.at[early], held.at[me, early, pl.ds(1, 4)]),
        load(4, top_rhs_hbm.at[0], top_rhs.at[row]),
    ]
    next_loads = [
        load(5, diag_hbm.at[late], held.at[me, late, 0]),
        load(6, off_hbm.at[late], held.at[me, late, pl.ds(1, 4)]),
    ]
    rhs_load = load(7, rhs_hbm, rhs)

    barrier = pltpu.get_barrier_semaphore()
    for peer in peers:
        pl.semaphore_signal(barrier, inc=1, device_id=(peer, me), device_id_type=MESH)
    pl.semaphore_signal(barrier, inc=1, device_id=(row, targets_of[ACROSS]), device_id_type=MESH)

    @pl.when(z > 0)
    def _():
        pl.semaphore_signal(barrier, inc=1, device_id=(row, targets_of[LEFT]), device_id_type=MESH)

    @pl.when(z < LINE - 1)
    def _():
        pl.semaphore_signal(barrier, inc=1, device_id=(row, targets_of[RIGHT]), device_id_type=MESH)

    for copy in first_loads + next_loads + [rhs_load]:
        copy.start()

    def clear(c, carry):
        acc[c] = jnp.zeros((width, columns), jnp.float32)
        return carry

    lax.fori_loop(0, cand, clear, 0)
    for u in range(CHUNK):
        prod[u * 5 + 4] = jnp.zeros((width, columns), jnp.float32)

    ends = jnp.where(z == 0, 1, 0) + jnp.where(z == LINE - 1, 1, 0)
    pl.semaphore_wait(barrier, rows + 2 - ends)
    for copy in first_loads:
        copy.wait()

    def row_copy(kind, p, src, dst):
        return pltpu.make_async_remote_copy(
            src_ref=src, dst_ref=dst, send_sem=row_send.at[kind, p], recv_sem=row_recv.at[kind, row],
            device_id=(peers[p], me), device_id_type=MESH,
        )

    def row_arrival(kind, p, dst):
        return pltpu.make_async_remote_copy(
            src_ref=dst, dst_ref=dst, send_sem=row_send.at[kind, p], recv_sem=row_recv.at[kind, peers[p]],
            device_id=(peers[p], me), device_id_type=MESH,
        )

    for p in range(rows - 1):
        row_copy(0, p, top_rhs.at[row], top_rhs.at[row]).start()

    def either(k, src, count, act):
        @pl.when(k == 0)
        def _():
            act(held_top.at[row, pl.ds(src, count)])

        @pl.when(k > 0)
        def _():
            act(held.at[pl.ds(src, count), pl.ds((k - 1) * CHUNK, CHUNK)])

    def describe(ref, k, src, way):
        return pltpu.make_async_remote_copy(
            src_ref=ref, dst_ref=ref, send_sem=send_sem.at[way, k], recv_sem=recv_sem.at[k, src],
            device_id=(row, targets_of[way]), device_id_type=MESH,
        )

    def relay(k, src, wait, ways):
        def act(ref):
            if wait:
                describe(ref, k, src, ACROSS).wait_recv()
            for way, wanted in ways:
                @pl.when(wanted)
                def _(way=way):
                    describe(ref, k, src, way).start()

        either(k, src, 1, act)

    def drain(k):
        around = detour(k)
        sends = {
            LEFT: jnp.where(z > 0, (LINE - z) * jnp.where(around, 2, 1), 0),
            RIGHT: jnp.where(z < LINE - 1, (z + 1) * jnp.where(around, 2, 1), 0),
            ACROSS: jnp.where(around, 1, LINE),
        }
        for way, sizes in ((LEFT, (1, 2, 3, 4, 6)), (RIGHT, (1, 2, 3, 4, 6)), (ACROSS, (1, LINE))):
            for size in sizes:
                @pl.when(sends[way] == size)
                def _(way=way, size=size):
                    either(k, 0, size, lambda ref: describe(ref, k, 0, way).wait_send())

    def solve(k):
        first = (k - 1) * CHUNK
        half = LEAF + LEAF // 2
        codes = [[targets[j, first + u] for j in range(4)] for u in range(CHUNK)]
        residuals = [
            (rhs[first + u].astype(jnp.float32) - acc[first + u]).astype(jnp.bfloat16) for u in range(CHUNK)
        ]
        solved = [
            jnp.dot(held[:, first + u, 0].reshape(width, width), residuals[u], preferred_element_type=jnp.float32)
            for u in range(CHUNK)
        ]
        solved = [x.astype(jnp.bfloat16) for x in solved]
        for u in range(CHUNK):
            sol[first + u] = solved[u]
        for u in range(CHUNK):
            blocks = [held[:, first + u, 1 + j].reshape(width, width) for j in range(4)]
            updates = jnp.dot(jnp.concatenate(blocks, axis=0), solved[u], preferred_element_type=jnp.float32)
            prod[pl.ds(u * 5, 4)] = updates.reshape(4, width, columns)
        pltpu.make_async_copy(sol.at[pl.ds(first, CHUNK)], out_hbm.at[pl.ds(first, CHUNK)], out_sem.at[0]).start()

        least = jnp.where(first < LEAF, LEAF, jnp.where(first < half, half, sub))

        def add(pair, carry):
            for c in (least + 2 * pair, least + 2 * pair + 1):
                total = acc[c]
                for u in range(CHUNK):
                    slot = jnp.int32(u * 5 + 4)
                    for j in range(4):
                        slot = jnp.where(codes[u][j] == c, u * 5 + j, slot)
                    total = total + prod[slot]
                acc[c] = total
            return carry

        lax.fori_loop(0, (cand - least) // 2, add, 0)

    def step(i, carry):
        for d in range(LINE):
            k = i - HOP * d

            @pl.when((k >= 0) & (k < chunks))
            def _(k=k, d=d):
                straight = jnp.logical_not(detour(k))
                if d == 0:
                    @pl.when(k == 2)
                    def _():
                        for copy in next_loads:
                            copy.wait()

                    relay(k, me, False, ((LEFT, z > 0), (RIGHT, z < LINE - 1), (ACROSS, z >= 0)))
                else:
                    @pl.when(z >= d)
                    def _():
                        relay(k, me - 2 * d, True, ((RIGHT, z < LINE - 1), (ACROSS, straight)))

                    @pl.when(z + d < LINE)
                    def _():
                        relay(k, me + 2 * d, True, ((LEFT, z > 0), (ACROSS, straight)))

            k = i - HOP * d - 1

            @pl.when((k >= 0) & (k < chunks) & detour(k))
            def _(k=k, d=d):
                far = targets_of[ACROSS]
                if d == 0:
                    relay(k, far, True, ((LEFT, z > 0), (RIGHT, z < LINE - 1)))
                else:
                    @pl.when(z >= d)
                    def _():
                        relay(k, far - 2 * d, True, ((RIGHT, z < LINE - 1),))

                    @pl.when(z + d < LINE)
                    def _():
                        relay(k, far + 2 * d, True, ((LEFT, z > 0),))

        k = i - READY

        @pl.when(k >= 0)
        def _():
            @pl.when(jnp.logical_not(detour(k)))
            def _():
                for other in range(LINE):
                    relay(k, other * 2 + 1 - y, True, ())

            @pl.when(k == 0)
            def _():
                rhs_load.wait()
                for p in range(rows - 1):
                    row_arrival(0, p, top_rhs.at[peers[p]]).wait_recv()
                for t in range(rows):
                    top_rhs_turned[t] = top_rhs[t].astype(jnp.float32).T
                for p in range(rows - 1):
                    row_copy(1, p, held_top.at[row], held_top.at[row]).start()

            @pl.when(k > 0)
            def _():
                solve(k)

            @pl.when(k == 1)
            def _():
                for p in range(rows - 1):
                    row_arrival(1, p, held_top.at[peers[p]]).wait_recv()

            for t in range(rows):
                @pl.when(k == t + 1)
                def _(t=t):
                    for block in range(t + 1):
                        full = held_top[t, :, block].reshape(width, width).astype(jnp.float32)
                        top_turned[t * 5 + block] = full.T.astype(jnp.bfloat16)

        @pl.when(i > READY)
        def _():
            drain(i - READY - 1)

        return carry

    steps = chunks + READY
    lax.fori_loop(0, steps, step, 0)

    mine = pl.ds(pl.multiple_of(row * share, share), share)
    for t in range(rows):
        turned[t] = acc[sub + t].T
        part[t] = turned[t].astype(jnp.bfloat16)
    slices = [part.at[:, pl.ds(pl.multiple_of(peer * share, share), share)] for peer in peers]
    for p in range(rows - 1):
        row_copy(2, p, slices[p], parts.at[row]).start()

    for p in range(rows - 1):
        row_arrival(2, p, parts.at[peers[p]]).wait_recv()

    def solved_copy(t):
        return pltpu.make_async_remote_copy(
            src_ref=top_sol.at[t], dst_ref=gathered.at[row], send_sem=top_send.at[t], recv_sem=top_recv.at[row],
            device_id=(t, me), device_id_type=MESH,
        )

    bases = []
    for t in range(rows):
        base = turned[t, mine]
        for p in range(rows - 1):
            base = base + parts[peers[p], t].astype(jnp.float32)
        bases.append(top_rhs_turned[t, mine] - base)
    for t in range(rows):
        x = jnp.dot(bases[t].astype(jnp.bfloat16), top_turned[t * 5], preferred_element_type=jnp.float32)
        x = x.astype(jnp.bfloat16)
        top_sol[t] = x
        for later in range(t + 1, rows):
            bases[later] = bases[later] - jnp.dot(
                x, top_turned[later * 5 + 1 + t], preferred_element_type=jnp.float32
            )
    for t in range(rows):
        @pl.when(row != t)
        def _(t=t):
            solved_copy(t).start()

        @pl.when(row == t)
        def _(t=t):
            gathered[row] = top_sol[t]

    for p in range(rows - 1):
        pltpu.make_async_remote_copy(
            src_ref=top_sol.at[0], dst_ref=gathered.at[peers[p]], send_sem=top_send.at[0], recv_sem=top_recv.at[peers[p]],
            device_id=(peers[p], me), device_id_type=MESH,
        ).wait_recv()
    owned = gathered[...].reshape(columns, width).astype(jnp.float32)
    top_out[...] = owned.T.astype(jnp.bfloat16)
    last = pltpu.make_async_copy(top_out, top_out_hbm.at[0], out_sem.at[1])
    last.start()
    def drain_rest(k, carry):
        drain(k)
        return carry

    lax.fori_loop(chunks - 1, chunks, drain_rest, 0)
    for p in range(rows - 1):
        row_copy(0, p, top_rhs.at[row], top_rhs.at[row]).wait_send()
        row_copy(1, p, held_top.at[row], held_top.at[row]).wait_send()
        row_copy(2, p, slices[p], parts.at[row]).wait_send()
    for t in range(rows):
        @pl.when(row != t)
        def _(t=t):
            solved_copy(t).wait_send()
    pltpu.make_async_copy(sol, out_hbm, out_sem.at[0]).wait()
    last.wait()


def place_kernel(local_in, top_in, local_out, top_out, local_held, top_held, in_sem, out_sem):
    pieces = len(range(0, local_in.shape[0], 2 * CHUNK))
    size = local_in.shape[0] // pieces
    parts = [pl.ds(index * size, size) for index in range(pieces)]
    stages = [(local_in.at[part], local_held.at[part], local_out.at[part]) for part in parts]
    stages.append((top_in, top_held, top_out))
    fetches = [pltpu.make_async_copy(a, b, in_sem.at[index]) for index, (a, b, c) in enumerate(stages)]
    stores = [pltpu.make_async_copy(b, c, out_sem.at[index]) for index, (a, b, c) in enumerate(stages)]
    for fetch in fetches:
        fetch.start()
    for fetch, store in zip(fetches, stores):
        fetch.wait()
        store.start()
    for store in stores:
        store.wait()


def placed(local_solution, top_solution):
    pieces = len(range(0, local_solution.shape[0], 2 * CHUNK))
    return pl.pallas_call(
        place_kernel,
        out_shape=tuple(jax.ShapeDtypeStruct(x.shape, x.dtype) for x in (local_solution, top_solution)),
        in_specs=[pl.BlockSpec(memory_space=pl.ANY)] * 2,
        out_specs=(pl.BlockSpec(memory_space=pl.ANY),) * 2,
        scratch_shapes=[
            pltpu.VMEM(local_solution.shape, local_solution.dtype),
            pltpu.VMEM(top_solution.shape, top_solution.dtype),
            pltpu.SemaphoreType.DMA((1 + pieces,)),
            pltpu.SemaphoreType.DMA((1 + pieces,)),
        ],
        compiler_params=pltpu.CompilerParams(vmem_limit_bytes=60 * 1024 * 1024),
    )(local_solution, top_solution)


def relayed(local_rhs, top_rhs, diag_inv, top_inv, off_blocks, top_factor, targets):
    rows, ranks = lax.axis_size("row"), lax.axis_size("rhs")
    sub, width, columns = local_rhs.shape
    share = diag_inv.shape[1]
    chunks = 1 + sub // CHUNK
    bf16, f32 = jnp.bfloat16, jnp.float32
    solutions = pl.pallas_call(
        functools.partial(relay_kernel, rows),
        out_shape=(
            jax.ShapeDtypeStruct(local_rhs.shape, bf16),
            jax.ShapeDtypeStruct(top_rhs.shape, bf16),
        ),
        in_specs=[pl.BlockSpec(memory_space=pltpu.HBM)] * 6 + [pl.BlockSpec(memory_space=pltpu.SMEM)],
        out_specs=(pl.BlockSpec(memory_space=pl.ANY),) * 2,
        scratch_shapes=[
            pltpu.VMEM((ranks, sub, 5, share, width), bf16),
            pltpu.VMEM((rows, ranks, 5, share, width), bf16),
            pltpu.VMEM((sub, width, columns), bf16),
            pltpu.VMEM((rows, width, columns), bf16),
            pltpu.VMEM((sub, width, columns), bf16),
            pltpu.VMEM((sub + rows, width, columns), f32),
            pltpu.VMEM((5 * CHUNK, width, columns), f32),
            pltpu.VMEM((rows, width, columns), bf16),
            pltpu.VMEM((rows, rows, columns // rows, width), bf16),
            pltpu.VMEM((rows, columns // rows, width), bf16),
            pltpu.VMEM((rows, columns, width), f32),
            pltpu.VMEM((rows, columns, width), f32),
            pltpu.VMEM((rows, columns // rows, width), bf16),
            pltpu.VMEM((width, columns), bf16),
            pltpu.VMEM((5 * rows, width, width), bf16),
            pltpu.SemaphoreType.DMA((8,)),
            pltpu.SemaphoreType.DMA((2,)),
            pltpu.SemaphoreType.DMA((3, chunks)),
            pltpu.SemaphoreType.DMA((chunks, ranks)),
            pltpu.SemaphoreType.DMA((3, rows - 1)),
            pltpu.SemaphoreType.DMA((3, rows)),
            pltpu.SemaphoreType.DMA((rows,)),
            pltpu.SemaphoreType.DMA((rows,)),
        ],
        compiler_params=pltpu.CompilerParams(
            collective_id=0, has_side_effects=True, vmem_limit_bytes=60 * 1024 * 1024
        ),
        cost_estimate=pl.CostEstimate(
            flops=10 * sub * width * width * columns, bytes_accessed=4 * local_rhs.size + 2 * off_blocks.size, transcendentals=0
        ),
    )(local_rhs, top_rhs, diag_inv, top_inv, off_blocks, top_factor, targets.T)
    return placed(*solutions)


def solution(mesh):
    in_specs = (
        P("row", None, "rhs"),
        P("row", None, "rhs"),
        P("row", "rhs", None),
        P("row", "rhs", None),
        P("row", None, "rhs", None),
        P("row", None, "rhs", None),
        P("row", None),
    )
    out_specs = (P("row", None, "rhs"), P("row", None, "rhs"))
    body = relayed if mesh.shape["rhs"] == 2 * LINE else local
    return jax.shard_map(body, mesh=mesh, in_specs=in_specs, out_specs=out_specs, check_vma=False)
```

```python
import functools
import jax
import jax.numpy as jnp
from jax import lax
from jax.experimental import pallas as pl
from jax.experimental.pallas import tpu as pltpu
from jax.sharding import PartitionSpec as P

LEAF = 24


def spread(shard, axis, root):
    mine = lax.axis_index(axis) == root
    return lax.psum(jnp.where(mine, shard, jnp.zeros_like(shard)), axis)


def local(local_rhs, top_rhs, diag_inv, top_inv, off_blocks, top_factor, targets):
    sub_count = local_rhs.shape[0]
    panel_width = local_rhs.shape[1]
    columns = local_rhs.shape[2]
    top_count = lax.axis_size("row")
    cand_count = sub_count + top_count
    acc_local = jnp.zeros((sub_count, panel_width, columns), jnp.float32)
    acc_top = jnp.zeros((top_count, panel_width, columns), jnp.float32)
    level_ranges = ((0, LEAF), (LEAF, LEAF + LEAF // 2), (LEAF + LEAF // 2, sub_count))
    solved = []
    for first_row, end_row in level_ranges:
        residual_rows = (
            local_rhs[first_row:end_row].astype(jnp.float32) - acc_local[first_row:end_row]
        ).astype(jnp.bfloat16)

        def apply_inverse(slice_part, offset, residual_rows=residual_rows):
            return jnp.einsum(
                "jxm,jme->jxe", slice_part, residual_rows, preferred_element_type=jnp.float32
            )

        level_partial = apply_inverse(
            lax.all_gather(diag_inv[first_row:end_row], "rhs", axis=1, tiled=True), jnp.int32(0)
        ).astype(jnp.bfloat16)
        solved.append(level_partial)
        target_codes = targets[first_row:end_row].reshape(-1)
        later_count = cand_count - end_row
        selector = (
            jnp.arange(later_count, dtype=jnp.int32)[:, None] == target_codes[None, :] - end_row
        ).astype(jnp.float32)

        def spread_updates(slice_part, offset, level_partial=level_partial, selector=selector):
            products = jnp.einsum(
                "yiko,yoq->yikq", slice_part, level_partial, preferred_element_type=jnp.float32
            )
            flattened = products.reshape(selector.shape[1], slice_part.shape[2], columns)
            return jnp.einsum("cn,nar->car", selector, flattened, precision=lax.Precision.HIGHEST)

        contrib = spread_updates(
            lax.all_gather(off_blocks[first_row:end_row], "rhs", axis=2, tiled=True), jnp.int32(0)
        )
        acc_local = acc_local.at[end_row:].add(contrib[: sub_count - end_row])
        acc_top = acc_top + contrib[sub_count - end_row :]
    inverse_rows = top_inv.reshape(1, 1, top_inv.shape[1], panel_width)
    top_full, inv_full = (
        lax.all_gather(top_factor, "rhs", axis=2, tiled=True),
        lax.all_gather(inverse_rows, "rhs", axis=2, tiled=True),
    )
    position = lax.axis_index("row")
    own_sum = lax.psum_scatter(
        acc_top.astype(jnp.bfloat16), "row", scatter_dimension=0, tiled=True
    ).astype(jnp.float32)
    base_value = top_rhs[0].astype(jnp.float32) - own_sum[0]

    def top_step(step_index, carry):
        carried, own_solution = carry
        residual_rows = (base_value - carried).astype(jnp.bfloat16)
        candidate = jnp.dot(
            inv_full[0, 0], residual_rows, preferred_element_type=jnp.float32
        ).astype(jnp.bfloat16)
        solution = spread(candidate, "row", step_index)
        own_solution = jnp.where(position == step_index, solution, own_solution)
        coupling_matrix = lax.dynamic_index_in_dim(top_full[0], step_index, 0, keepdims=False)
        update = jnp.dot(coupling_matrix, solution, preferred_element_type=jnp.float32)
        carried = carried + jnp.where(step_index < position, update, 0.0)
        return (carried, own_solution)

    initial_state = (
        jnp.zeros((panel_width, columns), jnp.float32),
        jnp.zeros((panel_width, columns), jnp.bfloat16),
    )
    own_separator = lax.fori_loop(0, top_count, top_step, initial_state)[1][None]
    return (jnp.concatenate(solved, axis=0), own_separator)


CHUNK = 3
LINE = 4
HOP = 1
READY = HOP * (LINE - 1) + 1
LEFT, RIGHT, ACROSS = 0, 1, 2
MESH = pl.DeviceIdType.MESH


def detour(k):
    return lax.rem(k, 6) == 4


def times_turned(left, right):
    return lax.dot_general(left, right, (((1,), (1,)), ((), ())), preferred_element_type=jnp.float32)


def relay_kernel(
    rows, rhs_hbm, top_rhs_hbm, diag_hbm, top_inv_hbm, off_hbm, top_factor_hbm, targets,
    out_hbm, top_out_hbm,
    held, held_top, rhs, top_rhs, sol, acc, prod, part, parts, top_sol,
    turned, top_rhs_turned, gathered, top_out,
    load_sem, out_sem, send_sem, recv_sem, row_send, row_recv, top_send, top_recv,
):
    sub, width, columns = rhs.shape
    chunks = 1 + sub // CHUNK
    cand = sub + rows
    share = columns // rows
    row, me = lax.axis_index("row"), lax.axis_index("rhs")
    z, y = me // 2, lax.rem(me, 2)
    targets_of = {LEFT: me - 2, RIGHT: me + 2, ACROSS: z * 2 + 1 - y}
    peers = [lax.rem(row + p, rows) for p in range(1, rows)]

    def load(index, src, dst):
        return pltpu.make_async_copy(src, dst, load_sem.at[index])

    early, late = pl.ds(0, CHUNK), pl.ds(CHUNK, sub - CHUNK)
    first_loads = [
        load(0, top_inv_hbm.at[0], held_top.at[row, me, 0]),
        load(1, top_factor_hbm.at[0], held_top.at[row, me, pl.ds(1, 4)]),
        load(2, diag_hbm.at[early], held.at[me, early, 0]),
        load(3, off_hbm.at[early], held.at[me, early, pl.ds(1, 4)]),
        load(4, top_rhs_hbm.at[0], top_rhs.at[row]),
    ]
    next_loads = [
        load(5, diag_hbm.at[late], held.at[me, late, 0]),
        load(6, off_hbm.at[late], held.at[me, late, pl.ds(1, 4)]),
    ]
    rhs_load = load(7, rhs_hbm, rhs)

    barrier = pltpu.get_barrier_semaphore()
    for peer in peers:
        pl.semaphore_signal(barrier, inc=1, device_id=(peer, me), device_id_type=MESH)
    pl.semaphore_signal(barrier, inc=1, device_id=(row, targets_of[ACROSS]), device_id_type=MESH)

    @pl.when(z > 0)
    def _():
        pl.semaphore_signal(barrier, inc=1, device_id=(row, targets_of[LEFT]), device_id_type=MESH)

    @pl.when(z < LINE - 1)
    def _():
        pl.semaphore_signal(barrier, inc=1, device_id=(row, targets_of[RIGHT]), device_id_type=MESH)

    for copy in first_loads + next_loads + [rhs_load]:
        copy.start()

    def clear(c, carry):
        acc[c] = jnp.zeros((width, columns), jnp.float32)
        return carry

    lax.fori_loop(0, cand, clear, 0)
    for u in range(CHUNK):
        prod[u * 5 + 4] = jnp.zeros((width, columns), jnp.float32)

    ends = jnp.where(z == 0, 1, 0) + jnp.where(z == LINE - 1, 1, 0)
    pl.semaphore_wait(barrier, rows + 2 - ends)
    for copy in first_loads:
        copy.wait()

    def row_copy(kind, p, src, dst):
        return pltpu.make_async_remote_copy(
            src_ref=src, dst_ref=dst, send_sem=row_send.at[kind, p], recv_sem=row_recv.at[kind, row],
            device_id=(peers[p], me), device_id_type=MESH,
        )

    def row_arrival(kind, p, dst):
        return pltpu.make_async_remote_copy(
            src_ref=dst, dst_ref=dst, send_sem=row_send.at[kind, p], recv_sem=row_recv.at[kind, peers[p]],
            device_id=(peers[p], me), device_id_type=MESH,
        )

    for p in range(rows - 1):
        row_copy(0, p, top_rhs.at[row], top_rhs.at[row]).start()

    def either(k, src, count, act):
        @pl.when(k == 0)
        def _():
            act(held_top.at[row, pl.ds(src, count)])

        @pl.when(k > 0)
        def _():
            act(held.at[pl.ds(src, count), pl.ds((k - 1) * CHUNK, CHUNK)])

    def describe(ref, k, src, way):
        return pltpu.make_async_remote_copy(
            src_ref=ref, dst_ref=ref, send_sem=send_sem.at[way, k], recv_sem=recv_sem.at[k, src],
            device_id=(row, targets_of[way]), device_id_type=MESH,
        )

    def relay(k, src, wait, ways):
        def act(ref):
            if wait:
                describe(ref, k, src, ACROSS).wait_recv()
            for way, wanted in ways:
                @pl.when(wanted)
                def _(way=way):
                    describe(ref, k, src, way).start()

        either(k, src, 1, act)

    def drain(k):
        around = detour(k)
        sends = {
            LEFT: jnp.where(z > 0, (LINE - z) * jnp.where(around, 2, 1), 0),
            RIGHT: jnp.where(z < LINE - 1, (z + 1) * jnp.where(around, 2, 1), 0),
            ACROSS: jnp.where(around, 1, LINE),
        }
        for way, sizes in ((LEFT, (1, 2, 3, 4, 6)), (RIGHT, (1, 2, 3, 4, 6)), (ACROSS, (1, LINE))):
            for size in sizes:
                @pl.when(sends[way] == size)
                def _(way=way, size=size):
                    either(k, 0, size, lambda ref: describe(ref, k, 0, way).wait_send())

    def solve(k):
        first = (k - 1) * CHUNK
        half = LEAF + LEAF // 2
        codes = [[targets[j, first + u] for j in range(4)] for u in range(CHUNK)]
        residuals = [
            (rhs[first + u].astype(jnp.float32) - acc[first + u]).astype(jnp.bfloat16) for u in range(CHUNK)
        ]
        solved = [
            jnp.dot(held[:, first + u, 0].reshape(width, width), residuals[u], preferred_element_type=jnp.float32)
            for u in range(CHUNK)
        ]
        solved = [x.astype(jnp.bfloat16) for x in solved]
        for u in range(CHUNK):
            sol[first + u] = solved[u]
        for u in range(CHUNK):
            blocks = [held[:, first + u, 1 + j].reshape(width, width) for j in range(4)]
            updates = jnp.dot(jnp.concatenate(blocks, axis=0), solved[u], preferred_element_type=jnp.float32)
            prod[pl.ds(u * 5, 4)] = updates.reshape(4, width, columns)
        pltpu.make_async_copy(sol.at[pl.ds(first, CHUNK)], out_hbm.at[pl.ds(first, CHUNK)], out_sem.at[0]).start()

        least = jnp.where(first < LEAF, LEAF, jnp.where(first < half, half, sub))

        def add(pair, carry):
            for c in (least + 2 * pair, least + 2 * pair + 1):
                total = acc[c]
                for u in range(CHUNK):
                    slot = jnp.int32(u * 5 + 4)
                    for j in range(4):
                        slot = jnp.where(codes[u][j] == c, u * 5 + j, slot)
                    total = total + prod[slot]
                acc[c] = total
            return carry

        lax.fori_loop(0, (cand - least) // 2, add, 0)

    def step(i, carry):
        for d in range(LINE):
            k = i - HOP * d

            @pl.when((k >= 0) & (k < chunks))
            def _(k=k, d=d):
                straight = jnp.logical_not(detour(k))
                if d == 0:
                    @pl.when(k == 2)
                    def _():
                        for copy in next_loads:
                            copy.wait()

                    relay(k, me, False, ((LEFT, z > 0), (RIGHT, z < LINE - 1), (ACROSS, z >= 0)))
                else:
                    @pl.when(z >= d)
                    def _():
                        relay(k, me - 2 * d, True, ((RIGHT, z < LINE - 1), (ACROSS, straight)))

                    @pl.when(z + d < LINE)
                    def _():
                        relay(k, me + 2 * d, True, ((LEFT, z > 0), (ACROSS, straight)))

            k = i - HOP * d - 1

            @pl.when((k >= 0) & (k < chunks) & detour(k))
            def _(k=k, d=d):
                far = targets_of[ACROSS]
                if d == 0:
                    relay(k, far, True, ((LEFT, z > 0), (RIGHT, z < LINE - 1)))
                else:
                    @pl.when(z >= d)
                    def _():
                        relay(k, far - 2 * d, True, ((RIGHT, z < LINE - 1),))

                    @pl.when(z + d < LINE)
                    def _():
                        relay(k, far + 2 * d, True, ((LEFT, z > 0),))

        k = i - READY

        @pl.when(k >= 0)
        def _():
            @pl.when(jnp.logical_not(detour(k)))
            def _():
                for other in range(LINE):
                    relay(k, other * 2 + 1 - y, True, ())

            @pl.when(k == 0)
            def _():
                rhs_load.wait()
                for p in range(rows - 1):
                    row_arrival(0, p, top_rhs.at[peers[p]]).wait_recv()
                for t in range(rows):
                    top_rhs_turned[t] = top_rhs[t].astype(jnp.float32).T
                for p in range(rows - 1):
                    row_copy(1, p, held_top.at[row], held_top.at[row]).start()

            @pl.when(k > 0)
            def _():
                solve(k)

        @pl.when(i > READY)
        def _():
            drain(i - READY - 1)

        return carry

    steps = chunks + READY
    lax.fori_loop(0, steps, step, 0)

    mine = pl.ds(pl.multiple_of(row * share, share), share)
    for t in range(rows):
        turned[t] = acc[sub + t].T
        part[t] = turned[t].astype(jnp.bfloat16)
    slices = [part.at[:, pl.ds(pl.multiple_of(peer * share, share), share)] for peer in peers]
    for p in range(rows - 1):
        row_copy(2, p, slices[p], parts.at[row]).start()

    for p in range(rows - 1):
        row_arrival(1, p, held_top.at[peers[p]]).wait_recv()
    for p in range(rows - 1):
        row_arrival(2, p, parts.at[peers[p]]).wait_recv()

    def solved_copy(t):
        return pltpu.make_async_remote_copy(
            src_ref=top_sol.at[t], dst_ref=gathered.at[row], send_sem=top_send.at[t], recv_sem=top_recv.at[row],
            device_id=(t, me), device_id_type=MESH,
        )

    for t in range(rows):
        base = turned[t, mine]
        for p in range(rows - 1):
            base = base + parts[peers[p], t].astype(jnp.float32)
        base = top_rhs_turned[t, mine] - base
        for earlier in range(t):
            factor = held_top[t, :, 1 + earlier].reshape(width, width)
            base = base - times_turned(top_sol[earlier], factor)
        inverse = held_top[t, :, 0].reshape(width, width)
        top_sol[t] = times_turned(base.astype(jnp.bfloat16), inverse).astype(jnp.bfloat16)

        @pl.when(row != t)
        def _(t=t):
            solved_copy(t).start()

        @pl.when(row == t)
        def _(t=t):
            gathered[row] = top_sol[t]

    for p in range(rows - 1):
        pltpu.make_async_remote_copy(
            src_ref=top_sol.at[0], dst_ref=gathered.at[peers[p]], send_sem=top_send.at[0], recv_sem=top_recv.at[peers[p]],
            device_id=(peers[p], me), device_id_type=MESH,
        ).wait_recv()
    owned = gathered[...].reshape(columns, width).astype(jnp.float32)
    top_out[...] = owned.T.astype(jnp.bfloat16)
    last = pltpu.make_async_copy(top_out, top_out_hbm.at[0], out_sem.at[1])
    last.start()
    def drain_rest(k, carry):
        drain(k)
        return carry

    lax.fori_loop(chunks - 1, chunks, drain_rest, 0)
    for p in range(rows - 1):
        row_copy(0, p, top_rhs.at[row], top_rhs.at[row]).wait_send()
        row_copy(1, p, held_top.at[row], held_top.at[row]).wait_send()
        row_copy(2, p, slices[p], parts.at[row]).wait_send()
    for t in range(rows):
        @pl.when(row != t)
        def _(t=t):
            solved_copy(t).wait_send()
    pltpu.make_async_copy(sol, out_hbm, out_sem.at[0]).wait()
    last.wait()


def place_kernel(local_in, top_in, local_out, top_out, local_held, top_held, in_sem, out_sem):
    pieces = len(range(0, local_in.shape[0], 2 * CHUNK))
    size = local_in.shape[0] // pieces
    parts = [pl.ds(index * size, size) for index in range(pieces)]
    stages = [(local_in.at[part], local_held.at[part], local_out.at[part]) for part in parts]
    stages.append((top_in, top_held, top_out))
    fetches = [pltpu.make_async_copy(a, b, in_sem.at[index]) for index, (a, b, c) in enumerate(stages)]
    stores = [pltpu.make_async_copy(b, c, out_sem.at[index]) for index, (a, b, c) in enumerate(stages)]
    for fetch in fetches:
        fetch.start()
    for fetch, store in zip(fetches, stores):
        fetch.wait()
        store.start()
    for store in stores:
        store.wait()


def placed(local_solution, top_solution):
    pieces = len(range(0, local_solution.shape[0], 2 * CHUNK))
    return pl.pallas_call(
        place_kernel,
        out_shape=tuple(jax.ShapeDtypeStruct(x.shape, x.dtype) for x in (local_solution, top_solution)),
        in_specs=[pl.BlockSpec(memory_space=pl.ANY)] * 2,
        out_specs=(pl.BlockSpec(memory_space=pl.ANY),) * 2,
        scratch_shapes=[
            pltpu.VMEM(local_solution.shape, local_solution.dtype),
            pltpu.VMEM(top_solution.shape, top_solution.dtype),
            pltpu.SemaphoreType.DMA((1 + pieces,)),
            pltpu.SemaphoreType.DMA((1 + pieces,)),
        ],
        compiler_params=pltpu.CompilerParams(vmem_limit_bytes=60 * 1024 * 1024),
    )(local_solution, top_solution)


def relayed(local_rhs, top_rhs, diag_inv, top_inv, off_blocks, top_factor, targets):
    rows, ranks = lax.axis_size("row"), lax.axis_size("rhs")
    sub, width, columns = local_rhs.shape
    share = diag_inv.shape[1]
    chunks = 1 + sub // CHUNK
    bf16, f32 = jnp.bfloat16, jnp.float32
    solutions = pl.pallas_call(
        functools.partial(relay_kernel, rows),
        out_shape=(
            jax.ShapeDtypeStruct(local_rhs.shape, bf16),
            jax.ShapeDtypeStruct(top_rhs.shape, bf16),
        ),
        in_specs=[pl.BlockSpec(memory_space=pltpu.HBM)] * 6 + [pl.BlockSpec(memory_space=pltpu.SMEM)],
        out_specs=(pl.BlockSpec(memory_space=pl.ANY),) * 2,
        scratch_shapes=[
            pltpu.VMEM((ranks, sub, 5, share, width), bf16),
            pltpu.VMEM((rows, ranks, 5, share, width), bf16),
            pltpu.VMEM((sub, width, columns), bf16),
            pltpu.VMEM((rows, width, columns), bf16),
            pltpu.VMEM((sub, width, columns), bf16),
            pltpu.VMEM((sub + rows, width, columns), f32),
            pltpu.VMEM((5 * CHUNK, width, columns), f32),
            pltpu.VMEM((rows, width, columns), bf16),
            pltpu.VMEM((rows, rows, columns // rows, width), bf16),
            pltpu.VMEM((rows, columns // rows, width), bf16),
            pltpu.VMEM((rows, columns, width), f32),
            pltpu.VMEM((rows, columns, width), f32),
            pltpu.VMEM((rows, columns // rows, width), bf16),
            pltpu.VMEM((width, columns), bf16),
            pltpu.SemaphoreType.DMA((8,)),
            pltpu.SemaphoreType.DMA((2,)),
            pltpu.SemaphoreType.DMA((3, chunks)),
            pltpu.SemaphoreType.DMA((chunks, ranks)),
            pltpu.SemaphoreType.DMA((3, rows - 1)),
            pltpu.SemaphoreType.DMA((3, rows)),
            pltpu.SemaphoreType.DMA((rows,)),
            pltpu.SemaphoreType.DMA((rows,)),
        ],
        compiler_params=pltpu.CompilerParams(
            collective_id=0, has_side_effects=True, vmem_limit_bytes=60 * 1024 * 1024
        ),
        cost_estimate=pl.CostEstimate(
            flops=10 * sub * width * width * columns, bytes_accessed=4 * local_rhs.size + 2 * off_blocks.size, transcendentals=0
        ),
    )(local_rhs, top_rhs, diag_inv, top_inv, off_blocks, top_factor, targets.T)
    return placed(*solutions)


def solution(mesh):
    in_specs = (
        P("row", None, "rhs"),
        P("row", None, "rhs"),
        P("row", "rhs", None),
        P("row", "rhs", None),
        P("row", None, "rhs", None),
        P("row", None, "rhs", None),
        P("row", None),
    )
    out_specs = (P("row", None, "rhs"), P("row", None, "rhs"))
    body = relayed if mesh.shape["rhs"] == 2 * LINE else local
    return jax.shard_map(body, mesh=mesh, in_specs=in_specs, out_specs=out_specs, check_vma=False)
```
